32 devices in a mesh: src: 4 (over z), tgt: 8 (over y, x, core).
Axes of the slice: x: 2, y: 2, z: 4, core: 2. Of those that a mesh axis runs over, the one named last changes fastest.
Arguments:
- src_emb: bfloat16 [8192, 1024], P(('src', 'tgt')), may hold values from 0 to 500, as said below
- tgt_emb: bfloat16 [4096, 1024], P('tgt'), may hold values from 0 to 500, as said below
- pair_list: int32 [32, 8], P('src'), may hold values from 0 to 15, as said below
- fwd_idx: int32 [8192, 16], P('src'), may hold values from 0 to 4095, as said below
- bwd_idx: int32 [4096, 16], P('tgt'), may hold values from 0 to 8191, as said below
Outputs:
- src_best: float32 [8192], P(('src', 'tgt'))
- tgt_best: float32 [4096], P('tgt')
The draws below stay inside these ranges and needn't reach their ends.
Inputs may be any that keep to these rules, and one draw needn't show every extreme that they name: src_emb entries are positive. tgt_emb entries are positive. `pair_list`: each row names 8 distinct target blocks in ascending order. Row b names block c whenever c mod 32 equals b, so every target block is named. All 2 blocks of one tgt index, the same for every row, are named in every row. `fwd_idx`: entry [i, k] is a target row of a block named in row i // 256 of pair_list; entries may repeat. `bwd_idx`: entry [j, k] is a source row of a block whose pair_list row names block j // 256; entries may repeat.
All inputs are finite; a program needn't handle non-finite values.
Results may differ from the reference program's by a relative error of at most 0.00091.
Values may be sent and summed in bfloat16 or wider, within the bound.
No kernel may reach another device: no remote copies, remote signals or barrier semaphores. Data moves between devices by JAX's collectives and lax.ppermute only.
A program may use at most 64 MiB of HBM per device.

```python
import jax
import jax.numpy as jnp
from jax import lax

D = 1024
BLOCK = 256
K = 16
P_SIZE = 8
TB_DEV = 2
NSB = 32
NTB = 16
NS = 8192
NT = 4096


def positive_rows(key, count):
    k_scale, k_value, k_band = jax.random.split(key, 3)
    spread = jnp.exp(jax.random.uniform(k_scale, (count, 1), jnp.float32, jnp.log(0.3), jnp.log(1.5)))
    values = jnp.clip(jax.random.normal(k_value, (count, D), jnp.float32), -2.6, 2.6)
    band_pick = jax.random.randint(k_band, (count, 1), 0, 8)
    feature_band = jnp.arange(D, dtype=jnp.int32) // (D // 8)
    boost = jnp.where(feature_band[None, :] == band_pick, 2.0, 0.0).astype(jnp.float32)
    return jnp.exp(spread * values + boost)


def pair_table(key):
    base = jax.random.fold_in(key, 11)
    k_owner, k_rank = jax.random.split(base)
    owner_index = jax.random.randint(k_owner, (), 0, NTB // TB_DEV)
    blocks = jnp.arange(NTB, dtype=jnp.int32)
    popular = (blocks // TB_DEV == owner_index).astype(jnp.int32)
    forced = (blocks[None, :] % NSB == jnp.arange(NSB, dtype=jnp.int32)[:, None]).astype(jnp.int32)
    ranks = jax.vmap(lambda k: jax.random.permutation(k, NTB))(jax.random.split(k_rank, NSB)).astype(jnp.int32)
    scores = ranks + NTB * (forced + 2 * popular[None, :])
    top_scores, chosen = lax.top_k(scores, P_SIZE)
    return jnp.sort(chosen.astype(jnp.int32), axis=1)


def draw_src_emb(key, part):
    return positive_rows(jax.random.fold_in(key, 21), NS).astype(jnp.bfloat16)


def draw_tgt_emb(key, part):
    return positive_rows(jax.random.fold_in(key, 22), NT).astype(jnp.bfloat16)


def draw_pair_list(key, part):
    return pair_table(key)


def draw_fwd_idx(key, part):
    chosen = pair_table(key)
    k_slot, k_inner = jax.random.split(jax.random.fold_in(key, 12))
    slot_pick = jax.random.randint(k_slot, (NS, K), 0, P_SIZE)
    inner_row = jax.random.randint(k_inner, (NS, K), 0, BLOCK)
    home_block = jnp.arange(NS, dtype=jnp.int32) // BLOCK
    return (chosen[home_block[:, None], slot_pick] * BLOCK + inner_row).astype(jnp.int32)


def draw_bwd_idx(key, part):
    chosen = pair_table(key)
    listing = jnp.any(chosen[:, :, None] == jnp.arange(NTB, dtype=jnp.int32)[None, None, :], axis=1).astype(jnp.int32)
    running = jnp.cumsum(listing, axis=0)
    totals = running[NSB - 1]
    k_pick, k_inner = jax.random.split(jax.random.fold_in(key, 13))
    home_block = jnp.arange(NT, dtype=jnp.int32) // BLOCK
    choose = jax.random.randint(k_pick, (NT, K), 0, 1 << 20) % totals[home_block][:, None]
    column = running.T[home_block]
    source_block = jnp.sum((column[:, None, :] <= choose[:, :, None]).astype(jnp.int32), axis=2)
    inner_row = jax.random.randint(k_inner, (NT, K), 0, BLOCK)
    return (source_block * BLOCK + inner_row).astype(jnp.int32)


def setup_inputs(seed: int = 0) -> dict:
    keys = jax.random.split(jax.random.key(seed), 6)
    src_emb = draw_src_emb(jax.random.fold_in(keys[5], 71), 0)
    tgt_emb = draw_tgt_emb(jax.random.fold_in(keys[5], 71), 0)
    pair_list = draw_pair_list(jax.random.fold_in(keys[5], 71), 0)
    fwd_idx = draw_fwd_idx(jax.random.fold_in(keys[5], 71), 0)
    bwd_idx = draw_bwd_idx(jax.random.fold_in(keys[5], 71), 0)
    return {"src_emb": src_emb, "tgt_emb": tgt_emb, "pair_list": pair_list, "fwd_idx": fwd_idx, "bwd_idx": bwd_idx}


def unit_rows(values):
    wide = values.astype(jnp.float32)
    factor = lax.rsqrt(lax.optimization_barrier(jnp.sum(wide * wide, axis=1, keepdims=True)) + 1e-06)
    return (wide * factor).astype(jnp.bfloat16)

def reference(src_emb, tgt_emb, pair_list, fwd_idx, bwd_idx):
    src_unit = unit_rows(src_emb)
    tgt_unit = unit_rows(tgt_emb)
    src_blocks = src_unit.reshape(NSB, BLOCK, D)
    tgt_blocks = tgt_unit.reshape(NTB, BLOCK, D)

    def fwd_block(args):
        block_rows, near_rows = args
        near_vecs = tgt_unit[near_rows].astype(jnp.float32)
        return lax.optimization_barrier(jnp.sum(near_vecs * block_rows.astype(jnp.float32)[:, None, :], axis=(1, 2))) / K

    def bwd_block(args):
        block_rows, near_rows = args
        near_vecs = src_unit[near_rows].astype(jnp.float32)
        return lax.optimization_barrier(jnp.sum(near_vecs * block_rows.astype(jnp.float32)[:, None, :], axis=(1, 2))) / K
    fwd_mean = lax.map(fwd_block, (src_blocks, fwd_idx.reshape(NSB, BLOCK, K)))
    bwd_mean = lax.map(bwd_block, (tgt_blocks, bwd_idx.reshape(NTB, BLOCK, K)))

    def margins(carry, args):
        block_rows, listed, fwd_rows = args
        columns = tgt_blocks[listed].reshape(P_SIZE * BLOCK, D)
        scores = jnp.dot(block_rows, columns.T, preferred_element_type=jnp.float32)
        bwd_cols = bwd_mean[listed].reshape(P_SIZE * BLOCK)
        ratio = 2.0 * scores / (fwd_rows[:, None] + bwd_cols[None, :])
        carry = carry.at[listed].max(lax.optimization_barrier(jnp.max(ratio, axis=0)).reshape(P_SIZE, BLOCK))
        return (carry, lax.optimization_barrier(jnp.max(ratio, axis=1)))
    tgt_peak, src_peak = lax.scan(margins, jnp.zeros((NTB, BLOCK), jnp.float32), (src_blocks, pair_list, fwd_mean))
    return (src_peak.reshape(NS), tgt_peak.reshape(NT))
```

```python
import functools

import jax
import jax.numpy as jnp
from jax import lax
from jax.experimental import pallas as pl
from jax.experimental.pallas import tpu as pltpu
from jax.sharding import PartitionSpec as P

BLOCK = 256
LANES = 128
PAIR = 2 * BLOCK
ROWS_CONTRACT = (((1,), (1,)), ((), ()))
VMEM = pl.BlockSpec(memory_space=pltpu.VMEM)
SMEM = pl.BlockSpec(memory_space=pltpu.SMEM)


def unit_rows(values):
    wide = values.astype(jnp.float32)
    factor = lax.rsqrt(jnp.sum(wide * wide, axis=1, keepdims=True) + 1e-06)
    return (wide * factor).astype(jnp.bfloat16)


def params(flops, bytes_accessed, **more):
    return dict(
        compiler_params=pltpu.CompilerParams(vmem_limit_bytes=32 * 2**20, **more),
        cost_estimate=pl.CostEstimate(flops=flops, bytes_accessed=bytes_accessed, transcendentals=0),
    )


def prepare_kernel(
    slots, own_ref, sibling_ref, pairs_ref, fwd_ref, bwd_own_ref, bwd_sibling_ref, unit_ref, fwd_at_ref, bwd_at_ref, listed_ref
):
    src_pos = lax.axis_index("src")
    tgt_pos = lax.axis_index("tgt")
    tgt_count = lax.axis_size("tgt")
    rows = own_ref.shape[0]

    def normalise(ref, base):
        def step(i, _):
            at = pl.multiple_of(i * 64, 64)
            unit_ref[pl.ds(base + at, 64), :] = unit_rows(ref[pl.ds(at, 64), :])
            return 0

        lax.fori_loop(0, rows // 64, step, 0)

    normalise(own_ref, 0)
    normalise(sibling_ref, rows)

    for group in range(fwd_at_ref.shape[0]):
        parts = []
        for g in range(8):
            slot, half = (group * 8 + g) // 2, g % 2
            first = lax.bitwise_xor(tgt_pos, 2 * slot) * BLOCK + half * LANES
            parts.append(fwd_ref[:, pl.ds(pl.multiple_of(first, LANES), LANES)])
        near = jnp.concatenate(parts, axis=0)
        chip = lax.bitwise_xor(near // rows, tgt_pos)
        at = jnp.where(chip < 2, chip * rows + near % rows, -1)
        fwd_at_ref[group] = at.T
    tiles = rows // LANES
    for group in range(bwd_at_ref.shape[0]):
        parts = []
        for g in range(8):
            tile = group * 8 + g
            ref = bwd_own_ref if tile < tiles else bwd_sibling_ref
            parts.append(ref[:, (tile % tiles) * LANES : (tile % tiles + 1) * LANES])
        near = jnp.concatenate(parts, axis=0)
        block = near // BLOCK - src_pos * tgt_count
        inside = (block >= 0) & (block < tgt_count)
        peer = lax.bitwise_xor(jnp.where(inside, block, 0), tgt_pos)
        inside = inside & (lax.bitwise_and(peer, 1) == 0)
        at = jnp.where(inside, (peer // 2) * BLOCK + near % BLOCK, -1)
        bwd_at_ref[group] = at.T
    blocks = 2 * rows // BLOCK
    for slot in range(slots):
        row = lax.bitwise_xor(tgt_pos, 2 * slot)
        named = [pairs_ref[row, k] for k in range(pairs_ref.shape[1])]
        for p in range(blocks):
            owner = lax.bitwise_xor(tgt_pos, p // (blocks // 2))
            block = owner * (blocks // 2) + p % (blocks // 2)
            hit = jnp.int32(0)
            for name in named:
                hit = hit | (name == block).astype(jnp.int32)
            listed_ref[slot * blocks + p] = hit


def score_kernel(slot, finish, halves, *refs):
    chunk_refs = refs[:halves]
    unit_ref, fwd_at_ref, bwd_at_ref = refs[halves : halves + 3]
    if finish:
        fwd_before, bwd_before = refs[halves + 3 : halves + 5]
        scores_ref, fwd_ref, bwd_ref, turned_ref, fwd_got, bwd_got = refs[halves + 5 :]
    else:
        scores_ref, fwd_ref, bwd_ref, turned_ref, fwd_got, bwd_got = refs[halves + 3 :]
    unit = jnp.concatenate([unit_rows(ref[...]) for ref in chunk_refs], axis=0)
    scores_ref[...] = lax.dot_general(unit, unit_ref[...], ROWS_CONTRACT, preferred_element_type=jnp.float32)
    turned_ref[...] = lax.dot_general(unit_ref[...], unit, ROWS_CONTRACT, preferred_element_type=jnp.float32)
    columns = unit_ref.shape[0] // LANES
    lane_tile = lax.broadcasted_iota(jnp.int32, (8, LANES), 1) // 16

    def gather(q, _):
        at = pl.multiple_of(q * 8, 8)
        near = fwd_at_ref[(2 * slot) // 8, pl.ds(at, 8), :]
        low, high = near & (LANES - 1), near >> 7
        got = jnp.zeros((8, LANES), jnp.float32)
        for half in range(2):
            mine = jnp.where(lane_tile == (2 * slot + half) % 8, high, -1)
            for c in range(columns):
                piece = scores_ref[pl.ds(half * LANES + at, 8), c * LANES : (c + 1) * LANES]
                got = jnp.where(mine == c, jnp.take_along_axis(piece, low, axis=1), got)
        fwd_got[pl.ds(at, 8), :] = got
        for group in range(bwd_at_ref.shape[0]):
            near = bwd_at_ref[group, pl.ds(at, 8), :]
            low, high = near & (LANES - 1), near >> 7
            got = jnp.zeros((8, LANES), jnp.float32)
            for g in range(8):
                mine = jnp.where(lane_tile == g, high, -1)
                for c in range(2):
                    piece = turned_ref[pl.ds((group * 8 + g) * LANES + at, 8), c * LANES : (c + 1) * LANES]
                    got = jnp.where(mine == 2 * slot + c, jnp.take_along_axis(piece, low, axis=1), got)
            bwd_got[group, pl.ds(at, 8), :] = got
        return 0

    lax.fori_loop(0, LANES // 8, gather, 0, unroll=2)
    first = (2 * slot) % 8 * 16
    fwd = fwd_got[...].T[first : first + 32].reshape(2, 16, LANES).sum(axis=1)
    bwd = [bwd_got[group].T.reshape(8, 16, LANES).sum(axis=1) for group in range(bwd_at_ref.shape[0])]
    bwd = bwd[0] if len(bwd) == 1 else jnp.concatenate(bwd, axis=0)
    if finish:
        before = fwd_before.shape[0]
        fwd_ref[:before, :] = fwd_before[...]
        fwd_ref[before:, :] = fwd
        bwd_ref[...] = bwd + bwd_before[...]
    else:
        fwd_ref[...] = fwd
        bwd_ref[...] = bwd


def margin_kernel(slots, columns, *refs):
    score_refs = refs[:slots]
    fwd_ref, bwd_ref, listed_ref, src_ref, tgt_ref, wide_ref, row_ref, col_ref = refs[slots:]
    blocks = columns // BLOCK
    row_ref[...] = jnp.zeros_like(row_ref)
    col_ref[...] = jnp.zeros_like(col_ref)
    for g in range(2 * slots):
        wide_ref[g * LANES : (g + 1) * LANES, :] = jnp.broadcast_to(fwd_ref[g : g + 1, :], (LANES, LANES)).T

    for slot in range(slots):
        scores_ref = score_refs[slot]

        def tile(p, _, slot=slot, scores_ref=scores_ref):
            @pl.when(listed_ref[slot * blocks + p] != 0)
            def _():
                bwd = [jnp.broadcast_to(bwd_ref[pl.ds(2 * p + c, 1), :], (8, LANES)) for c in range(2)]

                def rows(i, peak):
                    at = pl.multiple_of(i * 8, 8)
                    fwd = wide_ref[pl.ds(slot * BLOCK + at, 8), :]
                    best = row_ref[pl.ds(slot * BLOCK + at, 8), :]
                    peak = list(peak)
                    for c in range(2):
                        score = scores_ref[pl.ds(at, 8), pl.ds(pl.multiple_of(p * BLOCK + c * LANES, LANES), LANES)]
                        total = fwd + bwd[c]
                        inverse = pl.reciprocal(total, approx=True)
                        inverse = inverse * (2.0 - total * inverse)
                        ratio = score * inverse
                        best = jnp.maximum(best, ratio)
                        peak[c] = jnp.maximum(peak[c], ratio)
                    row_ref[pl.ds(slot * BLOCK + at, 8), :] = best
                    return tuple(peak)

                zero = jnp.zeros((8, LANES), jnp.float32)
                peak = lax.fori_loop(0, BLOCK // 8, rows, (zero, zero), unroll=8)
                for c in range(2):
                    where = pl.ds(pl.multiple_of(p * BLOCK + c * LANES, LANES), LANES)
                    col_ref[:, where] = jnp.maximum(col_ref[:, where], peak[c])

            return 0

        lax.fori_loop(0, blocks, tile, 0)
    for g in range(2 * slots):
        src_ref[g : g + 1, :] = 32.0 * jnp.max(row_ref[g * LANES : (g + 1) * LANES, :].T, axis=0, keepdims=True)
    for c in range(columns // LANES):
        tgt_ref[c : c + 1, :] = 32.0 * jnp.max(col_ref[:, c * LANES : (c + 1) * LANES], axis=0, keepdims=True)


def swap(value, axis, mask):
    count = lax.axis_size(axis)
    return lax.ppermute(value, axis, [(i, i ^ mask) for i in range(count)])


def turn_slots(value, bit):
    slots = value.shape[0] // 2
    return value.reshape(slots // (2 * bit), 2, bit * 2, LANES)[:, ::-1].reshape(value.shape)


def body(src_emb, tgt_emb, pair_list, fwd_idx, bwd_idx):
    tgt_count = lax.axis_size("tgt")
    src_count = lax.axis_size("src")
    slots = tgt_count // 2
    rows, width = tgt_emb.shape
    columns = 2 * rows
    tgt_bits = [1 << b for b in range(1, tgt_count.bit_length() - 1)]
    src_bits = [1 << b for b in range(src_count.bit_length() - 1)]

    upper, lower = src_emb[: BLOCK // 2], src_emb[BLOCK // 2 :]
    x_upper = swap(upper, "tgt", 2)
    y_lower = swap(lower, "tgt", 4)
    x_lower = swap(lower, "tgt", 2)
    y_upper = swap(upper, "tgt", 4)
    far_upper = swap(x_upper, "tgt", 4)
    far_lower = swap(y_lower, "tgt", 2)
    chunks = [(src_emb,), (x_upper, x_lower), (y_upper, y_lower), (far_upper, far_lower)]
    for bit in tgt_bits[2:]:
        chunks += [tuple(swap(part, "tgt", bit) for part in held) for held in chunks]

    sibling_emb = swap(tgt_emb, "tgt", 1)
    bwd_lists = bwd_idx.T
    sibling_lists = swap(bwd_lists, "tgt", 1)
    lists = jax.ShapeDtypeStruct((-(-slots // 4), LANES, LANES), jnp.int32)
    bwd_shape = jax.ShapeDtypeStruct((columns // (8 * LANES), LANES, LANES), jnp.int32)
    unit, fwd_at, bwd_at, listed = pl.pallas_call(
        functools.partial(prepare_kernel, slots),
        out_shape=(
            jax.ShapeDtypeStruct((columns, width), jnp.bfloat16),
            lists,
            bwd_shape,
            jax.ShapeDtypeStruct((slots * columns // BLOCK,), jnp.int32),
        ),
        in_specs=[VMEM, VMEM, SMEM, VMEM, VMEM, VMEM],
        out_specs=(VMEM, VMEM, VMEM, SMEM),
        name="prepare",
        **params(columns * width * 6, columns * width * 4),
    )(tgt_emb, sibling_emb, pair_list, fwd_idx.T, bwd_lists, sibling_lists)

    scores, fwd_parts, bwd_parts = [], [], []
    for slot in range(slots):
        finish = slot == slots - 1
        halves = len(chunks[slot])
        args = [*chunks[slot], unit, fwd_at, bwd_at]
        if finish:
            args += [jnp.concatenate(fwd_parts, axis=0), sum(bwd_parts[1:], bwd_parts[0])]
        score, fwd, bwd = pl.pallas_call(
            functools.partial(score_kernel, slot, finish, halves),
            out_shape=(
                jax.ShapeDtypeStruct((BLOCK, columns), jnp.float32),
                jax.ShapeDtypeStruct((2 * slots if finish else 2, LANES), jnp.float32),
                jax.ShapeDtypeStruct((columns // LANES, LANES), jnp.float32),
            ),
            in_specs=[VMEM] * len(args),
            out_specs=(VMEM, VMEM, VMEM),
            scratch_shapes=[
                pltpu.VMEM((columns, BLOCK), jnp.float32),
                pltpu.VMEM((LANES, LANES), jnp.float32),
                pltpu.VMEM(bwd_shape.shape, jnp.float32),
            ],
            name=f"score_{slot}",
            **params(4 * BLOCK * columns * width, BLOCK * columns * 4),
        )(*args)
        scores.append(score)
        fwd_parts.append(fwd)
        bwd_parts.append(bwd)

    def turn_pair(value):
        half = value.shape[0] // 2
        return jnp.concatenate([value[half:], value[:half]], axis=0)

    bwd = bwd + turn_pair(swap(bwd, "tgt", 1))
    for bit in tgt_bits:
        fwd = fwd + turn_slots(swap(fwd, "tgt", bit), bit // 2)
    for bit in src_bits:
        bwd = bwd + swap(bwd, "src", bit)

    src_best, tgt_best = pl.pallas_call(
        functools.partial(margin_kernel, slots, columns),
        out_shape=(
            jax.ShapeDtypeStruct((2 * slots, LANES), jnp.float32),
            jax.ShapeDtypeStruct((columns // LANES, LANES), jnp.float32),
        ),
        in_specs=[VMEM] * (slots + 2) + [SMEM],
        out_specs=(VMEM, VMEM),
        scratch_shapes=[
            pltpu.VMEM((slots * BLOCK, LANES), jnp.float32),
            pltpu.VMEM((slots * BLOCK, LANES), jnp.float32),
            pltpu.VMEM((8, columns), jnp.float32),
        ],
        name="margins",
        **params(slots * BLOCK * columns * 10, slots * BLOCK * columns * 4),
    )(*scores, fwd, bwd, listed)

    half = columns // LANES // 2
    tgt_best = jnp.maximum(tgt_best[:half], swap(tgt_best[half:], "tgt", 1))
    for bit in src_bits:
        tgt_best = jnp.maximum(tgt_best, swap(tgt_best, "src", bit))
    for bit in reversed(tgt_bits):
        keep = src_best.shape[0] // 2
        src_best = jnp.maximum(src_best[:keep], swap(src_best[keep:], "tgt", bit))
    return src_best.reshape(-1), tgt_best.reshape(-1)


def solution(mesh):
    return jax.shard_map(
        body,
        mesh=mesh,
        in_specs=(
            P(("src", "tgt"), None),
            P("tgt", None),
            P("src", None),
            P("src", None),
            P("tgt", None),
        ),
        out_specs=(P(("src", "tgt")), P("tgt")),
        check_vma=False,
    )
```

```python
import functools

import jax
import jax.numpy as jnp
from jax import lax
from jax.experimental import pallas as pl
from jax.experimental.pallas import tpu as pltpu
from jax.sharding import PartitionSpec as P

BLOCK = 256
LANES = 128
PAIR = 2 * BLOCK
ROWS_CONTRACT = (((1,), (1,)), ((), ()))
VMEM = pl.BlockSpec(memory_space=pltpu.VMEM)
SMEM = pl.BlockSpec(memory_space=pltpu.SMEM)


def unit_rows(values):
    wide = values.astype(jnp.float32)
    factor = lax.rsqrt(jnp.sum(wide * wide, axis=1, keepdims=True) + 1e-06)
    return (wide * factor).astype(jnp.bfloat16)


def params(flops, bytes_accessed, **more):
    return dict(
        compiler_params=pltpu.CompilerParams(vmem_limit_bytes=16 * 2**20, **more),
        cost_estimate=pl.CostEstimate(flops=flops, bytes_accessed=bytes_accessed, transcendentals=0),
    )


def normalise_kernel(own_ref, sibling_ref, unit_ref):
    rows = own_ref.shape[0]
    for i, ref in enumerate((own_ref, sibling_ref)):

        def step(j, _, i=i, ref=ref):
            at = pl.multiple_of(j * 64, 64)
            unit_ref[pl.ds(i * rows + at, 64), :] = unit_rows(ref[pl.ds(at, 64), :])
            return 0

        lax.fori_loop(0, rows // 64, step, 0)


def lists_kernel(slots, rows, pairs_ref, fwd_ref, bwd_own_ref, bwd_sibling_ref, fwd_at_ref, bwd_at_ref, listed_ref):
    src_pos = lax.axis_index("src")
    tgt_pos = lax.axis_index("tgt")
    tgt_count = lax.axis_size("tgt")
    for group in range(fwd_at_ref.shape[0]):
        parts = []
        for g in range(8):
            slot, half = (group * 8 + g) // 2, g % 2
            first = lax.bitwise_xor(tgt_pos, 2 * slot) * BLOCK + half * LANES
            parts.append(fwd_ref[:, pl.ds(pl.multiple_of(first, LANES), LANES)])
        near = jnp.concatenate(parts, axis=0)
        chip = lax.bitwise_xor(near // rows, tgt_pos)
        at = jnp.where(chip < 2, chip * rows + near % rows, -1)
        fwd_at_ref[group] = at.T
    tiles = rows // LANES
    for group in range(bwd_at_ref.shape[0]):
        parts = []
        for g in range(8):
            tile = group * 8 + g
            ref = bwd_own_ref if tile < tiles else bwd_sibling_ref
            parts.append(ref[:, (tile % tiles) * LANES : (tile % tiles + 1) * LANES])
        near = jnp.concatenate(parts, axis=0)
        block = near // BLOCK - src_pos * tgt_count
        inside = (block >= 0) & (block < tgt_count)
        peer = lax.bitwise_xor(jnp.where(inside, block, 0), tgt_pos)
        inside = inside & (lax.bitwise_and(peer, 1) == 0)
        at = jnp.where(inside, (peer // 2) * BLOCK + near % BLOCK, -1)
        bwd_at_ref[group] = at.T
    blocks = 2 * rows // BLOCK
    for slot in range(slots):
        row = lax.bitwise_xor(tgt_pos, 2 * slot)
        named = [pairs_ref[row, k] for k in range(pairs_ref.shape[1])]
        for p in range(blocks):
            owner = lax.bitwise_xor(tgt_pos, p // (blocks // 2))
            block = owner * (blocks // 2) + p % (blocks // 2)
            hit = jnp.int32(0)
            for name in named:
                hit = hit | (name == block).astype(jnp.int32)
            listed_ref[slot * blocks + p] = hit


def score_kernel(slot, earlier, halves, *refs):
    chunk_refs, refs = refs[:halves], refs[halves:]
    unit_ref, fwd_at_ref, bwd_at_ref, *refs = refs
    fwd_before, refs = refs[:earlier], refs[earlier:]
    bwd_before, refs = refs[:earlier], refs[earlier:]
    scores_ref, fwd_ref, bwd_ref, turned_ref, fwd_got, bwd_got = refs
    unit = jnp.concatenate([unit_rows(ref[...]) for ref in chunk_refs], axis=0)
    scores_ref[...] = lax.dot_general(unit, unit_ref[...], ROWS_CONTRACT, preferred_element_type=jnp.float32)
    turned_ref[...] = lax.dot_general(unit_ref[...], unit, ROWS_CONTRACT, preferred_element_type=jnp.float32)
    columns = unit_ref.shape[0] // LANES
    lane_tile = lax.broadcasted_iota(jnp.int32, (8, LANES), 1) // 16

    def gather(q, _):
        at = pl.multiple_of(q * 8, 8)
        near = fwd_at_ref[(2 * slot) // 8, pl.ds(at, 8), :]
        low, high = near & (LANES - 1), near >> 7
        got = jnp.zeros((8, LANES), jnp.float32)
        for half in range(2):
            mine = jnp.where(lane_tile == (2 * slot + half) % 8, high, -1)
            for c in range(columns):
                piece = scores_ref[pl.ds(half * LANES + at, 8), c * LANES : (c + 1) * LANES]
                got = jnp.where(mine == c, jnp.take_along_axis(piece, low, axis=1), got)
        fwd_got[pl.ds(at, 8), :] = got
        for group in range(bwd_at_ref.shape[0]):
            near = bwd_at_ref[group, pl.ds(at, 8), :]
            low, high = near & (LANES - 1), near >> 7
            got = jnp.zeros((8, LANES), jnp.float32)
            for g in range(8):
                mine = jnp.where(lane_tile == g, high, -1)
                for c in range(2):
                    piece = turned_ref[pl.ds((group * 8 + g) * LANES + at, 8), c * LANES : (c + 1) * LANES]
                    got = jnp.where(mine == 2 * slot + c, jnp.take_along_axis(piece, low, axis=1), got)
            bwd_got[group, pl.ds(at, 8), :] = got
        return 0

    lax.fori_loop(0, LANES // 8, gather, 0, unroll=2)
    first = (2 * slot) % 8 * 16
    fwd = fwd_got[...].T[first : first + 32].reshape(2, 16, LANES).sum(axis=1)
    bwd = [bwd_got[group].T.reshape(8, 16, LANES).sum(axis=1) for group in range(bwd_at_ref.shape[0])]
    bwd = bwd[0] if len(bwd) == 1 else jnp.concatenate(bwd, axis=0)
    for i, ref in enumerate(fwd_before):
        fwd_ref[2 * i : 2 * i + 2, :] = ref[...]
    for ref in bwd_before:
        bwd = bwd + ref[...]
    fwd_ref[2 * earlier :, :] = fwd
    bwd_ref[...] = bwd


def margin_kernel(slots, columns, *refs):
    score_refs = refs[:slots]
    fwd_ref, bwd_ref, listed_ref, src_ref, tgt_ref, wide_ref, row_ref, col_ref = refs[slots:]
    blocks = columns // BLOCK
    row_ref[...] = jnp.zeros_like(row_ref)
    col_ref[...] = jnp.zeros_like(col_ref)
    for g in range(2 * slots):
        wide_ref[g * LANES : (g + 1) * LANES, :] = jnp.broadcast_to(fwd_ref[g : g + 1, :], (LANES, LANES)).T

    for slot in range(slots):
        scores_ref = score_refs[slot]

        def tile(p, _, slot=slot, scores_ref=scores_ref):
            @pl.when(listed_ref[slot * blocks + p] != 0)
            def _():
                bwd = [jnp.broadcast_to(bwd_ref[pl.ds(2 * p + c, 1), :], (8, LANES)) for c in range(2)]

                def rows(i, peak):
                    at = pl.multiple_of(i * 8, 8)
                    fwd = wide_ref[pl.ds(slot * BLOCK + at, 8), :]
                    best = row_ref[pl.ds(slot * BLOCK + at, 8), :]
                    peak = list(peak)
                    for c in range(2):
                        score = scores_ref[pl.ds(at, 8), pl.ds(pl.multiple_of(p * BLOCK + c * LANES, LANES), LANES)]
                        total = fwd + bwd[c]
                        inverse = pl.reciprocal(total, approx=True)
                        inverse = inverse * (2.0 - total * inverse)
                        ratio = score * inverse
                        best = jnp.maximum(best, ratio)
                        peak[c] = jnp.maximum(peak[c], ratio)
                    row_ref[pl.ds(slot * BLOCK + at, 8), :] = best
                    return tuple(peak)

                zero = jnp.zeros((8, LANES), jnp.float32)
                peak = lax.fori_loop(0, BLOCK // 8, rows, (zero, zero), unroll=8)
                for c in range(2):
                    where = pl.ds(pl.multiple_of(p * BLOCK + c * LANES, LANES), LANES)
                    col_ref[:, where] = jnp.maximum(col_ref[:, where], peak[c])

            return 0

        lax.fori_loop(0, blocks, tile, 0)
    for g in range(2 * slots):
        src_ref[g : g + 1, :] = 32.0 * jnp.max(row_ref[g * LANES : (g + 1) * LANES, :].T, axis=0, keepdims=True)
    for c in range(columns // LANES):
        tgt_ref[c : c + 1, :] = 32.0 * jnp.max(col_ref[:, c * LANES : (c + 1) * LANES], axis=0, keepdims=True)


def swap(value, axis, mask):
    count = lax.axis_size(axis)
    return lax.ppermute(value, axis, [(i, i ^ mask) for i in range(count)])


def turn_slots(value, bit):
    slots = value.shape[0] // 2
    return value.reshape(slots // (2 * bit), 2, bit * 2, LANES)[:, ::-1].reshape(value.shape)


def body(src_emb, tgt_emb, pair_list, fwd_idx, bwd_idx):
    tgt_count = lax.axis_size("tgt")
    src_count = lax.axis_size("src")
    slots = tgt_count // 2
    rows, width = tgt_emb.shape
    columns = 2 * rows
    tgt_bits = [1 << b for b in range(1, tgt_count.bit_length() - 1)]
    src_bits = [1 << b for b in range(src_count.bit_length() - 1)]

    along_x = swap(src_emb, "tgt", 2)
    along_y = swap(src_emb, "tgt", 4)

    sibling_emb = swap(tgt_emb, "tgt", 1)
    bwd_lists = bwd_idx.T
    sibling_lists = swap(bwd_lists, "tgt", 1)

    unit = pl.pallas_call(
        normalise_kernel,
        out_shape=jax.ShapeDtypeStruct((columns, width), jnp.bfloat16),
        in_specs=[VMEM, VMEM],
        out_specs=VMEM,
        name="normalise",
        **params(1000, 1000),
    )(tgt_emb, sibling_emb)
    bwd_shape = jax.ShapeDtypeStruct((columns // (8 * LANES), LANES, LANES), jnp.int32)
    fwd_at, bwd_at, listed = pl.pallas_call(
        functools.partial(lists_kernel, slots, rows),
        out_shape=(
            jax.ShapeDtypeStruct((-(-slots // 4), LANES, LANES), jnp.int32),
            bwd_shape,
            jax.ShapeDtypeStruct((slots * columns // BLOCK,), jnp.int32),
        ),
        in_specs=[SMEM, VMEM, VMEM, VMEM],
        out_specs=(VMEM, VMEM, SMEM),
        name="lists",
        **params(1000, 1000),
    )(pair_list, fwd_idx.T, bwd_lists, sibling_lists)

    def score(slot, blocks, before=()):
        args = [*blocks, unit, fwd_at, bwd_at, *before]
        return pl.pallas_call(
            functools.partial(score_kernel, slot, len(before) // 2, len(blocks)),
            out_shape=(
                jax.ShapeDtypeStruct((BLOCK, columns), jnp.float32),
                jax.ShapeDtypeStruct((len(before) + 2, LANES), jnp.float32),
                jax.ShapeDtypeStruct((columns // LANES, LANES), jnp.float32),
            ),
            in_specs=[VMEM] * len(args),
            out_specs=(VMEM, VMEM, VMEM),
            scratch_shapes=[
                pltpu.VMEM((columns, BLOCK), jnp.float32),
                pltpu.VMEM((LANES, LANES), jnp.float32),
                pltpu.VMEM(bwd_shape.shape, jnp.float32),
            ],
            name=f"score_{slot}",
            **(params(4 * BLOCK * columns * width, BLOCK * columns * 4) if slot else params(1000, 1000)),
        )(*args)

    done = [score(0, (src_emb,))]
    along_x, along_y, *done[0] = lax.optimization_barrier((along_x, along_y, *done[0]))
    far_upper = swap(along_x[: BLOCK // 2], "tgt", 4)
    far_lower = swap(along_y[BLOCK // 2 :], "tgt", 2)
    blocks = [(src_emb,), (along_x,), (along_y,), (far_upper, far_lower)]
    for bit in tgt_bits[2:]:
        blocks += [tuple(swap(part, "tgt", bit) for part in held) for held in blocks]
    for slot in range(1, slots):
        before = ()
        if slot == slots - 1:
            before = [d[1] for d in done] + [d[2] for d in done]
        done.append(score(slot, blocks[slot], before))
    scores = [d[0] for d in done]
    fwd, bwd = done[-1][1:]
    def turn_pair(value):
        half = value.shape[0] // 2
        return jnp.concatenate([value[half:], value[:half]], axis=0)

    bwd = bwd + turn_pair(swap(bwd, "tgt", 1))
    for bit in tgt_bits:
        fwd = fwd + turn_slots(swap(fwd, "tgt", bit), bit // 2)
    for bit in src_bits:
        bwd = bwd + swap(bwd, "src", bit)

    src_best, tgt_best = pl.pallas_call(
        functools.partial(margin_kernel, slots, columns),
        out_shape=(
            jax.ShapeDtypeStruct((2 * slots, LANES), jnp.float32),
            jax.ShapeDtypeStruct((columns // LANES, LANES), jnp.float32),
        ),
        in_specs=[VMEM] * (slots + 2) + [SMEM],
        out_specs=(VMEM, VMEM),
        scratch_shapes=[
            pltpu.VMEM((slots * BLOCK, LANES), jnp.float32),
            pltpu.VMEM((slots * BLOCK, LANES), jnp.float32),
            pltpu.VMEM((8, columns), jnp.float32),
        ],
        name="margins",
        **params(slots * BLOCK * columns * 10, slots * BLOCK * columns * 4),
    )(*scores, fwd, bwd, listed)

    half = columns // LANES // 2
    tgt_best = jnp.maximum(tgt_best[:half], swap(tgt_best[half:], "tgt", 1))
    for bit in src_bits:
        tgt_best = jnp.maximum(tgt_best, swap(tgt_best, "src", bit))
    for bit in reversed(tgt_bits):
        keep = src_best.shape[0] // 2
        src_best = jnp.maximum(src_best[:keep], swap(src_best[keep:], "tgt", bit))
    return src_best.reshape(-1), tgt_best.reshape(-1)


def solution(mesh):
    return jax.shard_map(
        body,
        mesh=mesh,
        in_specs=(
            P(("src", "tgt"), None),
            P("tgt", None),
            P("src", None),
            P("src", None),
            P("tgt", None),
        ),
        out_specs=(P(("src", "tgt")), P("tgt")),
        check_vma=False,
    )
```

```python
import functools

import jax
import jax.numpy as jnp
from jax import lax
from jax.experimental import pallas as pl
from jax.experimental.pallas import tpu as pltpu
from jax.sharding import PartitionSpec as P

BLOCK = 256
LANES = 128
PAIR = 2 * BLOCK
ROWS_CONTRACT = (((1,), (1,)), ((), ()))
VMEM = pl.BlockSpec(memory_space=pltpu.VMEM)
SMEM = pl.BlockSpec(memory_space=pltpu.SMEM)


def unit_rows(values):
    wide = values.astype(jnp.float32)
    factor = lax.rsqrt(jnp.sum(wide * wide, axis=1, keepdims=True) + 1e-06)
    return (wide * factor).astype(jnp.bfloat16)


def params(flops, bytes_accessed):
    return dict(
        compiler_params=pltpu.CompilerParams(vmem_limit_bytes=16 * 2**20),
        cost_estimate=pl.CostEstimate(flops=flops, bytes_accessed=bytes_accessed, transcendentals=0),
    )


def prepare_kernel(
    slots, own_ref, sibling_ref, pairs_ref, fwd_ref, bwd_own_ref, bwd_sibling_ref, unit_ref, fwd_at_ref, bwd_at_ref, listed_ref
):
    src_pos = lax.axis_index("src")
    tgt_pos = lax.axis_index("tgt")
    tgt_count = lax.axis_size("tgt")
    rows = own_ref.shape[0]

    def normalise(ref, base):
        def step(i, _):
            at = pl.multiple_of(i * BLOCK, BLOCK)
            unit_ref[pl.ds(base + at, BLOCK), :] = unit_rows(ref[pl.ds(at, BLOCK), :])
            return 0

        lax.fori_loop(0, rows // BLOCK, step, 0)

    normalise(own_ref, 0)
    normalise(sibling_ref, rows)
    for group in range(fwd_at_ref.shape[0]):
        parts = []
        for g in range(8):
            slot, half = (group * 8 + g) // 2, g % 2
            first = lax.bitwise_xor(tgt_pos, 2 * slot) * BLOCK + half * LANES
            parts.append(fwd_ref[:, pl.ds(pl.multiple_of(first, LANES), LANES)])
        near = jnp.concatenate(parts, axis=0)
        chip = lax.bitwise_xor(near // rows, tgt_pos)
        at = jnp.where(chip < 2, chip * rows + near % rows, -1)
        fwd_at_ref[group] = at.T
    tiles = rows // LANES
    for group in range(bwd_at_ref.shape[0]):
        parts = []
        for g in range(8):
            tile = group * 8 + g
            ref = bwd_own_ref if tile < tiles else bwd_sibling_ref
            parts.append(ref[:, (tile % tiles) * LANES : (tile % tiles + 1) * LANES])
        near = jnp.concatenate(parts, axis=0)
        block = near // BLOCK - src_pos * tgt_count
        inside = (block >= 0) & (block < tgt_count)
        peer = lax.bitwise_xor(jnp.where(inside, block, 0), tgt_pos)
        inside = inside & (lax.bitwise_and(peer, 1) == 0)
        at = jnp.where(inside, (peer // 2) * BLOCK + near % BLOCK, -1)
        bwd_at_ref[group] = at.T
    blocks = 2 * rows // BLOCK
    for slot in range(slots):
        row = lax.bitwise_xor(tgt_pos, 2 * slot)
        named = [pairs_ref[row, k] for k in range(pairs_ref.shape[1])]
        for p in range(blocks):
            owner = lax.bitwise_xor(tgt_pos, p // (blocks // 2))
            block = owner * (blocks // 2) + p % (blocks // 2)
            hit = jnp.int32(0)
            for name in named:
                hit = hit | (name == block).astype(jnp.int32)
            listed_ref[slot * blocks + p] = hit


def score_kernel(slot, earlier, halves, *refs):
    chunk_refs, refs = refs[:halves], refs[halves:]
    unit_ref, fwd_at_ref, bwd_at_ref, *refs = refs
    fwd_before, refs = refs[:earlier], refs[earlier:]
    bwd_before, refs = refs[:earlier], refs[earlier:]
    scores_ref, fwd_ref, bwd_ref, turned_ref, fwd_got, bwd_got = refs
    unit = jnp.concatenate([unit_rows(ref[...]) for ref in chunk_refs], axis=0)
    scores_ref[...] = lax.dot_general(unit, unit_ref[...], ROWS_CONTRACT, preferred_element_type=jnp.float32)
    turned_ref[...] = lax.dot_general(unit_ref[...], unit, ROWS_CONTRACT, preferred_element_type=jnp.float32)
    columns = unit_ref.shape[0] // LANES
    lane_tile = lax.broadcasted_iota(jnp.int32, (8, LANES), 1) // 16

    def gather(at):
        near = fwd_at_ref[(2 * slot) // 8, pl.ds(at, 8), :]
        low, high = near & (LANES - 1), near >> 7
        got = jnp.zeros((8, LANES), jnp.float32)
        for half in range(2):
            mine = jnp.where(lane_tile == (2 * slot + half) % 8, high, -1)
            for c in range(columns):
                piece = scores_ref[pl.ds(half * LANES + at, 8), c * LANES : (c + 1) * LANES]
                got = jnp.where(mine == c, jnp.take_along_axis(piece, low, axis=1), got)
        fwd_got[pl.ds(at, 8), :] = got
        for group in range(bwd_at_ref.shape[0]):
            near = bwd_at_ref[group, pl.ds(at, 8), :]
            low, high = near & (LANES - 1), near >> 7
            got = jnp.zeros((8, LANES), jnp.float32)
            for g in range(8):
                mine = jnp.where(lane_tile == g, high, -1)
                for c in range(2):
                    piece = turned_ref[pl.ds((group * 8 + g) * LANES + at, 8), c * LANES : (c + 1) * LANES]
                    got = jnp.where(mine == 2 * slot + c, jnp.take_along_axis(piece, low, axis=1), got)
            bwd_got[group, pl.ds(at, 8), :] = got

    for q in range(LANES // 8):
        gather(q * 8)
    first = (2 * slot) % 8 * 16
    fwd = fwd_got[...].T[first : first + 32].reshape(2, 16, LANES).sum(axis=1)
    bwd = [bwd_got[group].T.reshape(8, 16, LANES).sum(axis=1) for group in range(bwd_at_ref.shape[0])]
    bwd = bwd[0] if len(bwd) == 1 else jnp.concatenate(bwd, axis=0)
    for i, ref in enumerate(fwd_before):
        fwd_ref[2 * i : 2 * i + 2, :] = ref[...]
    for ref in bwd_before:
        bwd = bwd + ref[...]
    fwd_ref[2 * earlier :, :] = fwd
    bwd_ref[...] = bwd


def margin_kernel(slots, columns, *refs):
    score_refs = refs[:slots]
    fwd_ref, bwd_ref, listed_ref, src_ref, tgt_ref, wide_ref, row_ref, col_ref = refs[slots:]
    blocks = columns // BLOCK
    row_ref[...] = jnp.zeros_like(row_ref)
    col_ref[...] = jnp.zeros_like(col_ref)
    for g in range(2 * slots):
        wide_ref[g * LANES : (g + 1) * LANES, :] = jnp.broadcast_to(fwd_ref[g : g + 1, :], (LANES, LANES)).T

    for slot in range(slots):
        scores_ref = score_refs[slot]

        def tile(p, _, slot=slot, scores_ref=scores_ref):
            @pl.when(listed_ref[slot * blocks + p] != 0)
            def _():
                bwd = [jnp.broadcast_to(bwd_ref[pl.ds(2 * p + c, 1), :], (8, LANES)) for c in range(2)]

                def rows(i, peak):
                    at = pl.multiple_of(i * 8, 8)
                    fwd = wide_ref[pl.ds(slot * BLOCK + at, 8), :]
                    best = row_ref[pl.ds(slot * BLOCK + at, 8), :]
                    peak = list(peak)
                    for c in range(2):
                        score = scores_ref[pl.ds(at, 8), pl.ds(pl.multiple_of(p * BLOCK + c * LANES, LANES), LANES)]
                        total = fwd + bwd[c]
                        inverse = pl.reciprocal(total, approx=True)
                        inverse = inverse * (2.0 - total * inverse)
                        ratio = score * inverse
                        best = jnp.maximum(best, ratio)
                        peak[c] = jnp.maximum(peak[c], ratio)
                    row_ref[pl.ds(slot * BLOCK + at, 8), :] = best
                    return tuple(peak)

                zero = jnp.zeros((8, LANES), jnp.float32)
                peak = lax.fori_loop(0, BLOCK // 8, rows, (zero, zero), unroll=8)
                for c in range(2):
                    where = pl.ds(pl.multiple_of(p * BLOCK + c * LANES, LANES), LANES)
                    col_ref[:, where] = jnp.maximum(col_ref[:, where], peak[c])

            return 0

        lax.fori_loop(0, blocks, tile, 0)
    for g in range(2 * slots):
        src_ref[g : g + 1, :] = 32.0 * jnp.max(row_ref[g * LANES : (g + 1) * LANES, :].T, axis=0, keepdims=True)
    for c in range(columns // LANES):
        tgt_ref[c : c + 1, :] = 32.0 * jnp.max(col_ref[:, c * LANES : (c + 1) * LANES], axis=0, keepdims=True)


def swap(value, axis, mask):
    count = lax.axis_size(axis)
    return lax.ppermute(value, axis, [(i, i ^ mask) for i in range(count)])


def turn_slots(value, bit):
    slots = value.shape[0] // 2
    return value.reshape(slots // (2 * bit), 2, bit * 2, LANES)[:, ::-1].reshape(value.shape)


def body(src_emb, tgt_emb, pair_list, fwd_idx, bwd_idx):
    tgt_count = lax.axis_size("tgt")
    src_count = lax.axis_size("src")
    slots = tgt_count // 2
    rows, width = tgt_emb.shape
    columns = 2 * rows
    tgt_bits = [1 << b for b in range(1, tgt_count.bit_length() - 1)]
    src_bits = [1 << b for b in range(src_count.bit_length() - 1)]

    along_x = swap(src_emb, "tgt", 2)
    along_y = swap(src_emb, "tgt", 4)

    sibling_emb = swap(tgt_emb, "tgt", 1)
    bwd_lists = bwd_idx.T
    sibling_lists = swap(bwd_lists, "tgt", 1)

    bwd_shape = jax.ShapeDtypeStruct((columns // (8 * LANES), LANES, LANES), jnp.int32)
    unit, fwd_at, bwd_at, listed = pl.pallas_call(
        functools.partial(prepare_kernel, slots),
        out_shape=(
            jax.ShapeDtypeStruct((columns, width), jnp.bfloat16),
            jax.ShapeDtypeStruct((-(-slots // 4), LANES, LANES), jnp.int32),
            bwd_shape,
            jax.ShapeDtypeStruct((slots * columns // BLOCK,), jnp.int32),
        ),
        in_specs=[VMEM, VMEM, SMEM, VMEM, VMEM, VMEM],
        out_specs=(VMEM, VMEM, VMEM, SMEM),
        name="prepare",
        **params(1000, 1000),
    )(tgt_emb, sibling_emb, pair_list, fwd_idx.T, bwd_lists, sibling_lists)

    def score(slot, blocks, before=()):
        args = [*blocks, unit, fwd_at, bwd_at, *before]
        return pl.pallas_call(
            functools.partial(score_kernel, slot, len(before) // 2, len(blocks)),
            out_shape=(
                pltpu.VMEM((BLOCK, columns), jnp.float32),
                jax.ShapeDtypeStruct((len(before) + 2, LANES), jnp.float32),
                jax.ShapeDtypeStruct((columns // LANES, LANES), jnp.float32),
            ),
            in_specs=[VMEM] * len(args),
            out_specs=(VMEM, VMEM, VMEM),
            scratch_shapes=[
                pltpu.VMEM((columns, BLOCK), jnp.float32),
                pltpu.VMEM((LANES, LANES), jnp.float32),
                pltpu.VMEM(bwd_shape.shape, jnp.float32),
            ],
            name=f"score_{slot}",
            **(params(4 * BLOCK * columns * width, BLOCK * columns * 4) if slot else params(1000, 1000)),
        )(*args)

    done = [score(0, (src_emb,))]
    along_x, along_y, *done[0] = lax.optimization_barrier((along_x, along_y, *done[0]))
    far_upper = swap(along_x[: BLOCK // 2], "tgt", 4)
    far_lower = swap(along_y[BLOCK // 2 :], "tgt", 2)
    blocks = [(src_emb,), (along_x,), (along_y,), (far_upper, far_lower)]
    for bit in tgt_bits[2:]:
        blocks += [tuple(swap(part, "tgt", bit) for part in held) for held in blocks]
    for slot in range(1, slots):
        before = ()
        if slot == slots - 1:
            before = [d[1] for d in done] + [d[2] for d in done]
        done.append(score(slot, blocks[slot], before))
    scores = [d[0] for d in done]
    fwd, bwd = done[-1][1:]
    def turn_pair(value):
        half = value.shape[0] // 2
        return jnp.concatenate([value[half:], value[:half]], axis=0)

    bwd = bwd + turn_pair(swap(bwd, "tgt", 1))
    for bit in tgt_bits:
        fwd = fwd + turn_slots(swap(fwd, "tgt", bit), bit // 2)
    for bit in src_bits:
        bwd = bwd + swap(bwd, "src", bit)

    src_best, tgt_best = pl.pallas_call(
        functools.partial(margin_kernel, slots, columns),
        out_shape=(
            jax.ShapeDtypeStruct((2 * slots, LANES), jnp.float32),
            jax.ShapeDtypeStruct((columns // LANES, LANES), jnp.float32),
        ),
        in_specs=[VMEM] * (slots + 2) + [SMEM],
        out_specs=(VMEM, VMEM),
        scratch_shapes=[
            pltpu.VMEM((slots * BLOCK, LANES), jnp.float32),
            pltpu.VMEM((slots * BLOCK, LANES), jnp.float32),
            pltpu.VMEM((8, columns), jnp.float32),
        ],
        name="margins",
        **params(slots * BLOCK * columns * 10, slots * BLOCK * columns * 4),
    )(*scores, fwd, bwd, listed)

    half = columns // LANES // 2
    tgt_best = jnp.maximum(tgt_best[:half], swap(tgt_best[half:], "tgt", 1))
    for bit in src_bits:
        tgt_best = jnp.maximum(tgt_best, swap(tgt_best, "src", bit))
    for bit in reversed(tgt_bits):
        keep = src_best.shape[0] // 2
        src_best = jnp.maximum(src_best[:keep], swap(src_best[keep:], "tgt", bit))
    return src_best.reshape(-1), tgt_best.reshape(-1)


def solution(mesh):
    return jax.shard_map(
        body,
        mesh=mesh,
        in_specs=(
            P(("src", "tgt"), None),
            P("tgt", None),
            P("src", None),
            P("src", None),
            P("tgt", None),
        ),
        out_specs=(P(("src", "tgt")), P("tgt")),
        check_vma=False,
    )
```

```python
import functools

import jax
import jax.numpy as jnp
from jax import lax
from jax.experimental import pallas as pl
from jax.experimental.pallas import tpu as pltpu
from jax.sharding import PartitionSpec as P

BLOCK = 256
LANES = 128
FIRST = 144
ROWS_CONTRACT = (((1,), (1,)), ((), ()))
VMEM = pl.BlockSpec(memory_space=pltpu.VMEM)
SMEM = pl.BlockSpec(memory_space=pltpu.SMEM)


def unit_rows(values):
    wide = values.astype(jnp.float32)
    factor = lax.rsqrt(jnp.sum(wide * wide, axis=1, keepdims=True) + 1e-06)
    return (wide * factor).astype(jnp.bfloat16)


def params(flops, bytes_accessed):
    return dict(
        compiler_params=pltpu.CompilerParams(vmem_limit_bytes=16 * 2**20),
        cost_estimate=pl.CostEstimate(flops=flops, bytes_accessed=bytes_accessed, transcendentals=0),
    )


def cut_kernel(emb_ref, second_ref, first_ref):
    second_ref[...] = emb_ref[: BLOCK - FIRST, :]
    first_ref[...] = emb_ref[BLOCK - FIRST :, :]


def normalise_kernel(emb_ref, unit_ref):
    def step(i, _):
        at = pl.multiple_of(i * BLOCK, BLOCK)
        unit_ref[pl.ds(at, BLOCK), :] = unit_rows(emb_ref[pl.ds(at, BLOCK), :])
        return 0

    lax.fori_loop(0, emb_ref.shape[0] // BLOCK, step, 0)


def prepare_kernel(
    slots, own_ref, pairs_ref, fwd_ref, bwd_own_ref, bwd_sibling_ref, unit_ref, fwd_at_ref, bwd_at_ref, listed_ref
):
    src_pos = lax.axis_index("src")
    tgt_pos = lax.axis_index("tgt")
    tgt_count = lax.axis_size("tgt")
    rows = own_ref.shape[0]
    normalise_kernel(own_ref, unit_ref)
    for group in range(fwd_at_ref.shape[0]):
        parts = []
        for g in range(8):
            slot, half = (group * 8 + g) // 2, g % 2
            first = lax.bitwise_xor(tgt_pos, 2 * slot) * BLOCK + half * LANES
            parts.append(fwd_ref[:, pl.ds(pl.multiple_of(first, LANES), LANES)])
        near = jnp.concatenate(parts, axis=0)
        chip = lax.bitwise_xor(near // rows, tgt_pos)
        at = jnp.where(chip < 2, chip * rows + near % rows, -1)
        fwd_at_ref[group] = at.T
    tiles = rows // LANES
    for group in range(bwd_at_ref.shape[0]):
        parts = []
        for g in range(8):
            tile = group * 8 + g
            ref = bwd_own_ref if tile < tiles else bwd_sibling_ref
            parts.append(ref[:, (tile % tiles) * LANES : (tile % tiles + 1) * LANES])
        near = jnp.concatenate(parts, axis=0)
        block = near // BLOCK - src_pos * tgt_count
        inside = (block >= 0) & (block < tgt_count)
        peer = lax.bitwise_xor(jnp.where(inside, block, 0), tgt_pos)
        inside = inside & (lax.bitwise_and(peer, 1) == 0)
        at = jnp.where(inside, (peer // 2) * BLOCK + near % BLOCK, -1)
        bwd_at_ref[group] = at.T
    blocks = 2 * rows // BLOCK
    for slot in range(slots):
        row = lax.bitwise_xor(tgt_pos, 2 * slot)
        named = [pairs_ref[row, k] for k in range(pairs_ref.shape[1])]
        for p in range(blocks):
            owner = lax.bitwise_xor(tgt_pos, p // (blocks // 2))
            block = owner * (blocks // 2) + p % (blocks // 2)
            hit = jnp.int32(0)
            for name in named:
                hit = hit | (name == block).astype(jnp.int32)
            listed_ref[slot * blocks + p] = hit


def gather_lanes(near, mine, first, pieces, got):
    for c, piece in enumerate(pieces):
        got = jnp.where(mine == first + c, jnp.take_along_axis(piece, near & (LANES - 1), axis=1), got)
    return got


def lane_tiles():
    return lax.broadcasted_iota(jnp.int32, (8, LANES), 1) // 16


def forward_part(slot, unit, own_ref, sibling_ref, fwd_at_ref, scores_ref, got_ref):
    rows = own_ref.shape[0]
    for i, ref in enumerate((own_ref, sibling_ref)):
        scores_ref[:, i * rows : (i + 1) * rows] = lax.dot_general(
            unit, ref[...], ROWS_CONTRACT, preferred_element_type=jnp.float32
        )
    lane_tile = lane_tiles()
    for at in range(0, LANES, 8):
        near = fwd_at_ref[(2 * slot) // 8, at : at + 8, :]
        got = jnp.zeros((8, LANES), jnp.float32)
        for half in range(2):
            mine = jnp.where(lane_tile == (2 * slot + half) % 8, near >> 7, -1)
            row = half * LANES + at
            pieces = [scores_ref[row : row + 8, c : c + LANES] for c in range(0, 2 * rows, LANES)]
            got = gather_lanes(near, mine, 0, pieces, got)
        got_ref[at : at + 8, :] = got
    first = (2 * slot) % 8 * 16
    return got_ref[...].T[first : first + 32].reshape(2, 16, LANES).sum(axis=1)


def backward_part(slot, unit, own_ref, sibling_ref, bwd_at_ref, turned_ref, got_ref):
    rows = own_ref.shape[0]
    for i, ref in enumerate((own_ref, sibling_ref)):
        turned_ref[i * rows : (i + 1) * rows, :] = lax.dot_general(
            ref[...], unit, ROWS_CONTRACT, preferred_element_type=jnp.float32
        )
    lane_tile = lane_tiles()
    sums = []
    for group in range(bwd_at_ref.shape[0]):
        for at in range(0, LANES, 8):
            near = bwd_at_ref[group, at : at + 8, :]
            got = jnp.zeros((8, LANES), jnp.float32)
            for g in range(8):
                mine = jnp.where(lane_tile == g, near >> 7, -1)
                row = (group * 8 + g) * LANES + at
                pieces = [turned_ref[row : row + 8, c : c + LANES] for c in range(0, BLOCK, LANES)]
                got = gather_lanes(near, mine, 2 * slot, pieces, got)
            got_ref[at : at + 8, :] = got
        sums.append(got_ref[...].T.reshape(8, 16, LANES).sum(axis=1))
    return sums[0] if len(sums) == 1 else jnp.concatenate(sums, axis=0)


def score_kernel(slot, parts, own_ref, sibling_ref, fwd_at_ref, bwd_at_ref, *refs):
    chunk_refs = refs[:parts]
    scores_ref, fwd_ref, bwd_ref, turned_ref, got_ref, back_ref = refs[parts:]
    unit = jnp.concatenate([unit_rows(ref[...]) for ref in chunk_refs], axis=0)
    fwd_ref[...] = forward_part(slot, unit, own_ref, sibling_ref, fwd_at_ref, scores_ref, got_ref)
    bwd_ref[...] = backward_part(slot, unit, own_ref, sibling_ref, bwd_at_ref, turned_ref, back_ref)


def last_score_kernel(slot, parts, own_ref, sibling_ref, fwd_at_ref, bwd_at_ref, *refs):
    chunk_refs, refs = refs[:parts], refs[parts:]
    fwd_before, bwd_before = refs[:slot], refs[slot : 2 * slot]
    scores_ref, fwd_ref, bwd_ref, turned_ref, got_ref, back_ref = refs[2 * slot :]
    unit = jnp.concatenate([unit_rows(ref[...]) for ref in chunk_refs], axis=0)
    for i, ref in enumerate(fwd_before):
        fwd_ref[2 * i : 2 * i + 2, :] = ref[...]
    fwd_ref[2 * slot :, :] = forward_part(slot, unit, own_ref, sibling_ref, fwd_at_ref, scores_ref, got_ref)
    bwd = backward_part(slot, unit, own_ref, sibling_ref, bwd_at_ref, turned_ref, back_ref)
    for ref in bwd_before:
        bwd = bwd + ref[...]
    bwd_ref[...] = bwd


def widen_kernel(fwd_ref, wide_ref):
    for g in range(fwd_ref.shape[0]):
        wide_ref[g * LANES : (g + 1) * LANES, :] = jnp.broadcast_to(fwd_ref[g : g + 1, :], (LANES, LANES)).T


def margin_kernel(slots, columns, *refs):
    score_refs = refs[:slots]
    wide_ref, bwd_ref, listed_ref, row_ref, tgt_ref, col_ref = refs[slots:]
    blocks = columns // BLOCK
    row_ref[...] = jnp.zeros_like(row_ref)
    col_ref[...] = jnp.zeros_like(col_ref)

    for slot in range(slots):
        scores_ref = score_refs[slot]

        def tile(p, _, slot=slot, scores_ref=scores_ref):
            @pl.when(listed_ref[slot * blocks + p] != 0)
            def _():
                columns_at = [pl.ds(pl.multiple_of(p * BLOCK + c * LANES, LANES), LANES) for c in range(2)]
                bwd = [jnp.broadcast_to(bwd_ref[pl.ds(2 * p + c, 1), :], (8, LANES)) for c in range(2)]
                peak = [jnp.zeros((8, LANES), jnp.float32)] * 2
                for at in range(0, BLOCK, 8):
                    rows = slice(slot * BLOCK + at, slot * BLOCK + at + 8)
                    fwd = wide_ref[rows, :]
                    best = row_ref[rows, :]
                    for c in range(2):
                        total = fwd + bwd[c]
                        inverse = pl.reciprocal(total, approx=True)
                        inverse = inverse * (2.0 - total * inverse)
                        ratio = scores_ref[at : at + 8, columns_at[c]] * inverse
                        best = jnp.maximum(best, ratio)
                        peak[c] = jnp.maximum(peak[c], ratio)
                    row_ref[rows, :] = best
                for c in range(2):
                    col_ref[:, columns_at[c]] = jnp.maximum(col_ref[:, columns_at[c]], peak[c])

            return 0

        lax.fori_loop(0, blocks, tile, 0)
    for c in range(columns // LANES):
        tgt_ref[c : c + 1, :] = 32.0 * jnp.max(col_ref[:, c * LANES : (c + 1) * LANES], axis=0, keepdims=True)


def row_kernel(row_ref, src_ref):
    for g in range(src_ref.shape[0]):
        src_ref[g : g + 1, :] = 32.0 * jnp.max(row_ref[g * LANES : (g + 1) * LANES, :].T, axis=0, keepdims=True)


def swap(value, axis, mask):
    count = lax.axis_size(axis)
    return lax.ppermute(value, axis, [(i, i ^ mask) for i in range(count)])


def turn_slots(value, bit):
    step = 2 * bit
    order = [i ^ 1 for i in range(value.shape[0] // step)]
    return jnp.concatenate([value[i * step : (i + 1) * step] for i in order], axis=0)


def body(src_emb, tgt_emb, pair_list, fwd_idx, bwd_idx):
    tgt_count = lax.axis_size("tgt")
    src_count = lax.axis_size("src")
    slots = tgt_count // 2
    rows, width = tgt_emb.shape
    columns = 2 * rows
    tgt_bits = [1 << b for b in range(1, tgt_count.bit_length() - 1)]
    src_bits = [1 << b for b in range(src_count.bit_length() - 1)]

    along_x = swap(src_emb, "tgt", 2)
    second, first = pl.pallas_call(
        cut_kernel,
        out_shape=(
            jax.ShapeDtypeStruct((BLOCK - FIRST, width), src_emb.dtype),
            jax.ShapeDtypeStruct((FIRST, width), src_emb.dtype),
        ),
        in_specs=[VMEM],
        out_specs=(VMEM, VMEM),
        name="cut",
        **params(1000, 1000),
    )(src_emb)
    y_first = swap(first, "tgt", 4)

    sibling_emb = swap(tgt_emb, "tgt", 1)
    bwd_lists = bwd_idx.T
    sibling_lists = swap(bwd_lists, "tgt", 1)

    bwd_shape = jax.ShapeDtypeStruct((columns // (8 * LANES), LANES, LANES), jnp.int32)
    unit_shape = jax.ShapeDtypeStruct((rows, width), jnp.bfloat16)
    sibling_unit = pl.pallas_call(
        normalise_kernel,
        out_shape=unit_shape,
        in_specs=[VMEM],
        out_specs=VMEM,
        name="normalise",
        **params(10**9, rows * width * 4),
    )(sibling_emb)
    own_unit, fwd_at, bwd_at, listed = pl.pallas_call(
        functools.partial(prepare_kernel, slots),
        out_shape=(
            unit_shape,
            jax.ShapeDtypeStruct((-(-slots // 4), LANES, LANES), jnp.int32),
            bwd_shape,
            jax.ShapeDtypeStruct((slots * columns // BLOCK,), jnp.int32),
        ),
        in_specs=[VMEM, SMEM, VMEM, VMEM, VMEM],
        out_specs=(VMEM, VMEM, VMEM, SMEM),
        name="prepare",
        **params(1000, 1000),
    )(tgt_emb, pair_list, fwd_idx.T, bwd_lists, sibling_lists)

    scores_shape = jax.ShapeDtypeStruct((BLOCK, columns), jnp.float32)
    bwd_sums = jax.ShapeDtypeStruct((columns // LANES, LANES), jnp.float32)
    turned = pltpu.VMEM((columns, BLOCK), jnp.float32)
    got = pltpu.VMEM((LANES, LANES), jnp.float32)

    def score(slot, parts):
        args = [own_unit, sibling_unit, fwd_at, bwd_at, *parts]
        return pl.pallas_call(
            functools.partial(score_kernel, slot, len(parts)),
            out_shape=(scores_shape, jax.ShapeDtypeStruct((2, LANES), jnp.float32), bwd_sums),
            in_specs=[VMEM] * len(args),
            out_specs=(VMEM, VMEM, VMEM),
            scratch_shapes=[turned, got, got],
            name=f"score_{slot}",
            **(params(4 * BLOCK * columns * width, BLOCK * columns * 4) if slot else params(1000, 1000)),
        )(*args)

    second, own_unit, sibling_unit = lax.optimization_barrier((second, own_unit, sibling_unit))
    y_second = swap(second, "tgt", 4)
    done = [score(0, (src_emb,))]
    y_first, *done[0] = lax.optimization_barrier((y_first, *done[0]))
    far_first = swap(y_first, "tgt", 2)
    along_x, *done[0] = lax.optimization_barrier((along_x, *done[0]))
    far_second = swap(along_x[: BLOCK - FIRST], "tgt", 4)
    blocks = [(src_emb,), (along_x,), (y_second, y_first), (far_second, far_first)]
    for bit in tgt_bits[2:]:
        blocks += [tuple(swap(part, "tgt", bit) for part in held) for held in blocks]
    for slot in range(1, slots - 1):
        done.append(score(slot, blocks[slot]))
    args = [own_unit, sibling_unit, fwd_at, bwd_at, *blocks[-1], *(d[1] for d in done), *(d[2] for d in done)]
    last_scores, fwd, bwd = pl.pallas_call(
        functools.partial(last_score_kernel, slots - 1, len(blocks[-1])),
        out_shape=(scores_shape, jax.ShapeDtypeStruct((2 * slots, LANES), jnp.float32), bwd_sums),
        in_specs=[VMEM] * len(args),
        out_specs=(VMEM, VMEM, VMEM),
        scratch_shapes=[turned, got, got],
        name=f"score_{slots - 1}",
        **params(4 * BLOCK * columns * width, BLOCK * columns * 4),
    )(*args)
    scores = [*(d[0] for d in done), last_scores]

    def turn_pair(value):
        half = value.shape[0] // 2
        return jnp.concatenate([value[half:], value[:half]], axis=0)

    for bit in src_bits:
        bwd = bwd + swap(bwd, "src", bit)
    bwd = bwd + turn_pair(swap(bwd, "tgt", 1))
    for bit in tgt_bits:
        fwd = fwd + turn_slots(swap(fwd, "tgt", bit), bit // 2)

    wide_shape = jax.ShapeDtypeStruct((slots * BLOCK, LANES), jnp.float32)
    wide = pl.pallas_call(
        widen_kernel, out_shape=wide_shape, in_specs=[VMEM], out_specs=VMEM, name="widen", **params(10**6, 10**6)
    )(fwd)
    row_peaks, tgt_best = pl.pallas_call(
        functools.partial(margin_kernel, slots, columns),
        out_shape=(wide_shape, bwd_sums),
        in_specs=[VMEM] * (slots + 2) + [SMEM],
        out_specs=(VMEM, VMEM),
        scratch_shapes=[pltpu.VMEM((8, columns), jnp.float32)],
        name="margins",
        **params(slots * BLOCK * columns * 10, slots * BLOCK * columns * 4),
    )(*scores, wide, bwd, listed)
    src_best = pl.pallas_call(
        row_kernel,
        out_shape=jax.ShapeDtypeStruct((2 * slots, LANES), jnp.float32),
        in_specs=[VMEM],
        out_specs=VMEM,
        name="row_best",
        **params(10**6, 10**6),
    )(row_peaks)

    for bit in src_bits:
        tgt_best = jnp.maximum(tgt_best, swap(tgt_best, "src", bit))
    half = columns // LANES // 2
    tgt_best = jnp.maximum(tgt_best[:half], swap(tgt_best[half:], "tgt", 1))
    for bit in reversed(tgt_bits):
        keep = src_best.shape[0] // 2
        src_best = jnp.maximum(src_best[:keep], swap(src_best[keep:], "tgt", bit))
    return src_best.reshape(-1), tgt_best.reshape(-1)


def solution(mesh):
    return jax.shard_map(
        body,
        mesh=mesh,
        in_specs=(
            P(("src", "tgt"), None),
            P("tgt", None),
            P("src", None),
            P("src", None),
            P("tgt", None),
        ),
        out_specs=(P(("src", "tgt")), P("tgt")),
        check_vma=False,
    )
```

```python
import functools

import jax
import jax.numpy as jnp
from jax import lax
from jax.experimental import pallas as pl
from jax.experimental.pallas import tpu as pltpu
from jax.sharding import PartitionSpec as P

BLOCK = 256
LANES = 128
FIRST = 160
ROWS_CONTRACT = (((1,), (1,)), ((), ()))
VMEM = pl.BlockSpec(memory_space=pltpu.VMEM)
SMEM = pl.BlockSpec(memory_space=pltpu.SMEM)


def unit_rows(values):
    wide = values.astype(jnp.float32)
    factor = lax.rsqrt(jnp.sum(wide * wide, axis=1, keepdims=True) + 1e-06)
    return (wide * factor).astype(jnp.bfloat16)


def params(flops, bytes_accessed):
    return dict(
        compiler_params=pltpu.CompilerParams(vmem_limit_bytes=16 * 2**20),
        cost_estimate=pl.CostEstimate(flops=flops, bytes_accessed=bytes_accessed, transcendentals=0),
    )


def cut_kernel(emb_ref, second_ref, first_ref):
    second_ref[...] = emb_ref[: BLOCK - FIRST, :]
    first_ref[...] = emb_ref[BLOCK - FIRST :, :]


def normalise_kernel(emb_ref, unit_ref):
    def step(i, _):
        at = pl.multiple_of(i * BLOCK, BLOCK)
        unit_ref[pl.ds(at, BLOCK), :] = unit_rows(emb_ref[pl.ds(at, BLOCK), :])
        return 0

    lax.fori_loop(0, emb_ref.shape[0] // BLOCK, step, 0)


def prepare_kernel(
    slots, own_ref, pairs_ref, fwd_ref, bwd_own_ref, bwd_sibling_ref, unit_ref, fwd_at_ref, bwd_at_ref, listed_ref
):
    src_pos = lax.axis_index("src")
    tgt_pos = lax.axis_index("tgt")
    tgt_count = lax.axis_size("tgt")
    rows = own_ref.shape[0]
    normalise_kernel(own_ref, unit_ref)
    for group in range(fwd_at_ref.shape[0]):
        parts = []
        for g in range(8):
            slot, half = (group * 8 + g) // 2, g % 2
            first = lax.bitwise_xor(tgt_pos, 2 * slot) * BLOCK + half * LANES
            parts.append(fwd_ref[:, pl.ds(pl.multiple_of(first, LANES), LANES)])
        near = jnp.concatenate(parts, axis=0)
        chip = lax.bitwise_xor(near // rows, tgt_pos)
        at = jnp.where(chip < 2, chip * rows + near % rows, -1)
        fwd_at_ref[group] = at.T
    tiles = rows // LANES
    for group in range(bwd_at_ref.shape[0]):
        parts = []
        for g in range(8):
            tile = group * 8 + g
            ref = bwd_own_ref if tile < tiles else bwd_sibling_ref
            parts.append(ref[:, (tile % tiles) * LANES : (tile % tiles + 1) * LANES])
        near = jnp.concatenate(parts, axis=0)
        block = near // BLOCK - src_pos * tgt_count
        inside = (block >= 0) & (block < tgt_count)
        peer = lax.bitwise_xor(jnp.where(inside, block, 0), tgt_pos)
        inside = inside & (lax.bitwise_and(peer, 1) == 0)
        at = jnp.where(inside, (peer // 2) * BLOCK + near % BLOCK, -1)
        bwd_at_ref[group] = at.T
    blocks = 2 * rows // BLOCK
    for slot in range(slots):
        row = lax.bitwise_xor(tgt_pos, 2 * slot)
        named = [pairs_ref[row, k] for k in range(pairs_ref.shape[1])]
        for p in range(blocks):
            owner = lax.bitwise_xor(tgt_pos, p // (blocks // 2))
            block = owner * (blocks // 2) + p % (blocks // 2)
            hit = jnp.int32(0)
            for name in named:
                hit = hit | (name == block).astype(jnp.int32)
            listed_ref[slot * blocks + p] = hit


def gather_lanes(near, mine, first, pieces, got):
    for c, piece in enumerate(pieces):
        got = jnp.where(mine == first + c, jnp.take_along_axis(piece, near & (LANES - 1), axis=1), got)
    return got


def lane_tiles():
    return lax.broadcasted_iota(jnp.int32, (8, LANES), 1) // 16


def forward_part(slot, unit, own_ref, sibling_ref, fwd_at_ref, scores_ref, got_ref):
    rows = own_ref.shape[0]
    for i, ref in enumerate((own_ref, sibling_ref)):
        scores_ref[:, i * rows : (i + 1) * rows] = lax.dot_general(
            unit, ref[...], ROWS_CONTRACT, preferred_element_type=jnp.float32
        )
    lane_tile = lane_tiles()
    for at in range(0, LANES, 8):
        near = fwd_at_ref[(2 * slot) // 8, at : at + 8, :]
        got = jnp.zeros((8, LANES), jnp.float32)
        for half in range(2):
            mine = jnp.where(lane_tile == (2 * slot + half) % 8, near >> 7, -1)
            row = half * LANES + at
            pieces = [scores_ref[row : row + 8, c : c + LANES] for c in range(0, 2 * rows, LANES)]
            got = gather_lanes(near, mine, 0, pieces, got)
        got_ref[at : at + 8, :] = got
    first = (2 * slot) % 8 * 16
    return got_ref[...].T[first : first + 32].reshape(2, 16, LANES).sum(axis=1)


def backward_part(slot, unit, own_ref, sibling_ref, bwd_at_ref, turned_ref, got_ref):
    rows = own_ref.shape[0]
    for i, ref in enumerate((own_ref, sibling_ref)):
        turned_ref[i * rows : (i + 1) * rows, :] = lax.dot_general(
            ref[...], unit, ROWS_CONTRACT, preferred_element_type=jnp.float32
        )
    lane_tile = lane_tiles()
    sums = []
    for group in range(bwd_at_ref.shape[0]):
        for at in range(0, LANES, 8):
            near = bwd_at_ref[group, at : at + 8, :]
            got = jnp.zeros((8, LANES), jnp.float32)
            for g in range(8):
                mine = jnp.where(lane_tile == g, near >> 7, -1)
                row = (group * 8 + g) * LANES + at
                pieces = [turned_ref[row : row + 8, c : c + LANES] for c in range(0, BLOCK, LANES)]
                got = gather_lanes(near, mine, 2 * slot, pieces, got)
            got_ref[at : at + 8, :] = got
        sums.append(got_ref[...].T.reshape(8, 16, LANES).sum(axis=1))
    return sums[0] if len(sums) == 1 else jnp.concatenate(sums, axis=0)


def score_kernel(slot, parts, own_ref, sibling_ref, fwd_at_ref, bwd_at_ref, *refs):
    chunk_refs = refs[:parts]
    scores_ref, fwd_ref, bwd_ref, turned_ref, got_ref, back_ref = refs[parts:]
    unit = jnp.concatenate([unit_rows(ref[...]) for ref in chunk_refs], axis=0)
    fwd_ref[...] = forward_part(slot, unit, own_ref, sibling_ref, fwd_at_ref, scores_ref, got_ref)
    bwd_ref[...] = backward_part(slot, unit, own_ref, sibling_ref, bwd_at_ref, turned_ref, back_ref)


def last_score_kernel(slot, parts, own_ref, sibling_ref, fwd_at_ref, bwd_at_ref, *refs):
    chunk_refs, refs = refs[:parts], refs[parts:]
    fwd_before, bwd_before = refs[:slot], refs[slot : 2 * slot]
    scores_ref, fwd_ref, bwd_ref, send_ref, turned_ref, got_ref, back_ref = refs[2 * slot :]
    unit = jnp.concatenate([unit_rows(ref[...]) for ref in chunk_refs], axis=0)
    for i, ref in enumerate(fwd_before):
        fwd_ref[2 * i : 2 * i + 2, :] = ref[...]
    fwd_ref[2 * slot :, :] = forward_part(slot, unit, own_ref, sibling_ref, fwd_at_ref, scores_ref, got_ref)
    bwd = backward_part(slot, unit, own_ref, sibling_ref, bwd_at_ref, turned_ref, back_ref)
    for ref in bwd_before:
        bwd = bwd + ref[...]
    bwd_ref[...] = bwd
    send_ref[...] = choose(fwd_ref[...], bwd, send_ref.shape[0])


def fit(value, rows):
    if value.shape[0] < rows:
        value = jnp.concatenate([value, jnp.zeros((rows - value.shape[0], LANES), value.dtype)], axis=0)
    return value[:rows]


def choose(on_odd, on_even, rows):
    odd = lax.broadcasted_iota(jnp.int32, (rows, LANES), 0) * 0 + lax.axis_index("tgt") % 2 == 1
    return jnp.where(odd, fit(on_odd, rows), fit(on_even, rows))


def turn_pair(value):
    half = value.shape[0] // 2
    return jnp.concatenate([value[half:], value[:half]], axis=0)


def masks(slots):
    return [2, 1, *range(3, slots)]


def pair_kernel(combine, by_src_ref, by_tgt_ref, got_ref, state_ref):
    high, wide = by_src_ref.shape[0], by_tgt_ref.shape[0]
    by_src = jnp.concatenate([by_src_ref[...], got_ref[:high, :]], axis=0)
    by_tgt = combine(by_tgt_ref[...], turn_pair(got_ref[:wide, :]))
    state_ref[...] = choose(by_tgt, by_src, state_ref.shape[0])


def collect_kernel(combine, slots, wide, last, state_ref, *refs):
    got_refs, (total_ref, send_ref) = refs[:-2], refs[-2:]
    by_tgt = state_ref[:wide, :]
    by_src = [state_ref[2 * i : 2 * i + 2, :] for i in range(2 * slots)]
    for k, ref in enumerate(got_refs):
        by_tgt = combine(by_tgt, ref[:wide, :])
        if k + 1 < slots:
            order = [2 * (i ^ masks(slots)[k]) for i in range(2 * slots)]
            by_src = [combine(one, ref[i : i + 2, :]) for one, i in zip(by_src, order, strict=True)]
    by_src = jnp.concatenate(by_src, axis=0)
    total_ref[...] = choose(by_tgt, by_src, total_ref.shape[0])
    send_ref[...] = choose(by_tgt[wide // 2 :] if last else by_tgt, by_src[2 * slots :], send_ref.shape[0])


def widen_kernel(wide, total_ref, got_ref, wide_ref, bwd_ref):
    high = wide_ref.shape[0] // LANES
    fwd = choose(got_ref[:high, :], total_ref[:high, :], high)
    bwd_ref[...] = choose(total_ref[:wide, :], turn_pair(got_ref[:wide, :]), wide)
    for g in range(high):
        wide_ref[g * LANES : (g + 1) * LANES, :] = jnp.broadcast_to(fwd[g : g + 1, :], (LANES, LANES)).T


def margin_kernel(slots, columns, *refs):
    score_refs = refs[:slots]
    wide_ref, bwd_ref, listed_ref, src_ref, tgt_ref, send_ref, row_ref, col_ref = refs[slots:]
    blocks = columns // BLOCK
    row_ref[...] = jnp.zeros_like(row_ref)
    col_ref[...] = jnp.zeros_like(col_ref)

    for slot in range(slots):
        scores_ref = score_refs[slot]

        def tile(p, _, slot=slot, scores_ref=scores_ref):
            @pl.when(listed_ref[slot * blocks + p] != 0)
            def _():
                columns_at = [pl.ds(pl.multiple_of(p * BLOCK + c * LANES, LANES), LANES) for c in range(2)]
                bwd = [jnp.broadcast_to(bwd_ref[pl.ds(2 * p + c, 1), :], (8, LANES)) for c in range(2)]
                peak = [jnp.zeros((8, LANES), jnp.float32)] * 2
                for at in range(0, BLOCK, 8):
                    rows = slice(slot * BLOCK + at, slot * BLOCK + at + 8)
                    fwd = wide_ref[rows, :]
                    best = row_ref[rows, :]
                    for c in range(2):
                        total = fwd + bwd[c]
                        inverse = pl.reciprocal(total, approx=True)
                        inverse = inverse * (2.0 - total * inverse)
                        ratio = scores_ref[at : at + 8, columns_at[c]] * inverse
                        best = jnp.maximum(best, ratio)
                        peak[c] = jnp.maximum(peak[c], ratio)
                    row_ref[rows, :] = best
                for c in range(2):
                    col_ref[:, columns_at[c]] = jnp.maximum(col_ref[:, columns_at[c]], peak[c])

            return 0

        lax.fori_loop(0, blocks, tile, 0)
    for c in range(columns // LANES):
        tgt_ref[c : c + 1, :] = 32.0 * jnp.max(col_ref[:, c * LANES : (c + 1) * LANES], axis=0, keepdims=True)
    for g in range(src_ref.shape[0]):
        src_ref[g : g + 1, :] = 32.0 * jnp.max(row_ref[g * LANES : (g + 1) * LANES, :].T, axis=0, keepdims=True)
    send_ref[...] = choose(src_ref[...], tgt_ref[...], send_ref.shape[0])


def last_kernel(total_ref, got_ref, src_ref, tgt_ref):
    src, tgt = src_ref.shape[0], tgt_ref.shape[0]
    src_ref[...] = choose(got_ref[:src, :], total_ref[:src, :], src)
    tgt_ref[...] = choose(total_ref[:tgt, :], got_ref[:tgt, :], tgt)


def swap(value, axis, mask):
    count = lax.axis_size(axis)
    return lax.ppermute(value, axis, [(i, i ^ mask) for i in range(count)])


def small_call(kernel, name, shapes, *args):
    return pl.pallas_call(
        kernel,
        out_shape=tuple(jax.ShapeDtypeStruct((rows, LANES), jnp.float32) for rows in shapes),
        in_specs=[VMEM] * len(args),
        out_specs=(VMEM,) * len(shapes),
        name=name,
        **params(10**6, 10**6),
    )(*args)


def reduce_all(combine, by_src, by_tgt, send, name, last):
    tgt_count, src_count = lax.axis_size("tgt"), lax.axis_size("src")
    high, wide = by_src.shape[0], by_tgt.shape[0]
    got = swap(send, "tgt", 1)
    rows = max(2 * high, wide)
    (state,) = small_call(functools.partial(pair_kernel, combine), name + "_pair", (rows,), by_src, by_tgt, got)
    parts = []
    for i in range(1, max(tgt_count // 2, src_count)):
        pairs = []
        for device in range(src_count * tgt_count):
            if device % 2 == 0 and i < tgt_count // 2:
                pairs.append((device, device ^ (2 * masks(tgt_count // 2)[i - 1])))
            if device % 2 == 1 and i < src_count:
                pairs.append((device, device ^ (i * tgt_count)))
        parts.append(lax.ppermute(state, ("src", "tgt"), pairs))
    back = max(2, wide // 2) if last else max(high, wide)
    total, send = small_call(
        functools.partial(collect_kernel, combine, high // 2, wide, last), name + "_collect", (rows, back), state, *parts
    )
    return total, swap(send, "tgt", 1)


def body(src_emb, tgt_emb, pair_list, fwd_idx, bwd_idx):
    tgt_count = lax.axis_size("tgt")
    slots = tgt_count // 2
    rows, width = tgt_emb.shape
    columns = 2 * rows
    tgt_bits = [1 << b for b in range(1, tgt_count.bit_length() - 1)]

    along_x = swap(src_emb, "tgt", 2)
    second, first = pl.pallas_call(
        cut_kernel,
        out_shape=(
            jax.ShapeDtypeStruct((BLOCK - FIRST, width), src_emb.dtype),
            jax.ShapeDtypeStruct((FIRST, width), src_emb.dtype),
        ),
        in_specs=[VMEM],
        out_specs=(VMEM, VMEM),
        name="cut",
        **params(1000, 1000),
    )(src_emb)
    y_first = swap(first, "tgt", 4)

    sibling_emb = swap(tgt_emb, "tgt", 1)
    bwd_lists = bwd_idx.T
    sibling_lists = swap(bwd_lists, "tgt", 1)

    bwd_shape = jax.ShapeDtypeStruct((columns // (8 * LANES), LANES, LANES), jnp.int32)
    unit_shape = jax.ShapeDtypeStruct((rows, width), jnp.bfloat16)
    sibling_unit = pl.pallas_call(
        normalise_kernel,
        out_shape=unit_shape,
        in_specs=[VMEM],
        out_specs=VMEM,
        name="normalise",
        **params(10**9, rows * width * 4),
    )(sibling_emb)
    own_unit, fwd_at, bwd_at, listed = pl.pallas_call(
        functools.partial(prepare_kernel, slots),
        out_shape=(
            unit_shape,
            jax.ShapeDtypeStruct((-(-slots // 4), LANES, LANES), jnp.int32),
            bwd_shape,
            jax.ShapeDtypeStruct((slots * columns // BLOCK,), jnp.int32),
        ),
        in_specs=[VMEM, SMEM, VMEM, VMEM, VMEM],
        out_specs=(VMEM, VMEM, VMEM, SMEM),
        name="prepare",
        **params(1000, 1000),
    )(tgt_emb, pair_list, fwd_idx.T, bwd_lists, sibling_lists)

    scores_shape = jax.ShapeDtypeStruct((BLOCK, columns), jnp.float32)
    bwd_sums = jax.ShapeDtypeStruct((columns // LANES, LANES), jnp.float32)
    turned = pltpu.VMEM((columns, BLOCK), jnp.float32)
    got = pltpu.VMEM((LANES, LANES), jnp.float32)

    def score(slot, parts):
        args = [own_unit, sibling_unit, fwd_at, bwd_at, *parts]
        return pl.pallas_call(
            functools.partial(score_kernel, slot, len(parts)),
            out_shape=(scores_shape, jax.ShapeDtypeStruct((2, LANES), jnp.float32), bwd_sums),
            in_specs=[VMEM] * len(args),
            out_specs=(VMEM, VMEM, VMEM),
            scratch_shapes=[turned, got, got],
            name=f"score_{slot}",
            **(params(4 * BLOCK * columns * width, BLOCK * columns * 4) if slot else params(1000, 1000)),
        )(*args)

    own_unit, sibling_unit = lax.optimization_barrier((own_unit, sibling_unit))
    y_second = swap(second, "tgt", 4)
    done = [score(0, (src_emb,))]
    y_first, *done[0] = lax.optimization_barrier((y_first, *done[0]))
    far_first = swap(y_first, "tgt", 2)
    along_x, *done[0] = lax.optimization_barrier((along_x, *done[0]))
    far_second = swap(along_x[: BLOCK - FIRST], "tgt", 4)
    blocks = [(src_emb,), (along_x,), (y_second, y_first), (far_second, far_first)]
    for bit in tgt_bits[2:]:
        blocks += [tuple(swap(part, "tgt", bit) for part in held) for held in blocks]
    along_y = score(2, blocks[2])
    along_x, *along_y = lax.optimization_barrier((along_x, *along_y))
    done += [score(1, (along_x,)), along_y]
    for slot in range(3, slots - 1):
        done.append(score(slot, blocks[slot]))
    args = [own_unit, sibling_unit, fwd_at, bwd_at, *blocks[-1], *(d[1] for d in done), *(d[2] for d in done)]
    fwd_sums = jax.ShapeDtypeStruct((2 * slots, LANES), jnp.float32)
    sent = jax.ShapeDtypeStruct((max(2 * slots, columns // LANES), LANES), jnp.float32)
    last_scores, fwd, bwd, send = pl.pallas_call(
        functools.partial(last_score_kernel, slots - 1, len(blocks[-1])),
        out_shape=(scores_shape, fwd_sums, bwd_sums, sent),
        in_specs=[VMEM] * len(args),
        out_specs=(VMEM,) * 4,
        scratch_shapes=[turned, got, got],
        name=f"score_{slots - 1}",
        **params(4 * BLOCK * columns * width, BLOCK * columns * 4),
    )(*args)
    scores = [*(d[0] for d in done), last_scores]

    total, got = reduce_all(jnp.add, fwd, bwd, send, "mean", False)
    wide, bwd = small_call(
        functools.partial(widen_kernel, columns // LANES), "widen", (slots * BLOCK, columns // LANES), total, got
    )
    src_best, tgt_best, send = pl.pallas_call(
        functools.partial(margin_kernel, slots, columns),
        out_shape=(fwd_sums, bwd_sums, sent),
        in_specs=[VMEM] * (slots + 2) + [SMEM],
        out_specs=(VMEM,) * 3,
        scratch_shapes=[pltpu.VMEM((slots * BLOCK, LANES), jnp.float32), pltpu.VMEM((8, columns), jnp.float32)],
        name="margins",
        **params(slots * BLOCK * columns * 10, slots * BLOCK * columns * 4),
    )(*scores, wide, bwd, listed)
    total, got = reduce_all(jnp.maximum, src_best, tgt_best, send, "best", True)
    src_best, tgt_best = small_call(last_kernel, "last", (BLOCK // LANES, rows // LANES), total, got)
    return src_best.reshape(-1), tgt_best.reshape(-1)


def solution(mesh):
    return jax.shard_map(
        body,
        mesh=mesh,
        in_specs=(
            P(("src", "tgt"), None),
            P("tgt", None),
            P("src", None),
            P("src", None),
            P("tgt", None),
        ),
        out_specs=(P(("src", "tgt")), P("tgt")),
        check_vma=False,
    )
```

```python
import functools

import jax
import jax.numpy as jnp
from jax import lax
from jax.experimental import pallas as pl
from jax.experimental.pallas import tpu as pltpu
from jax.sharding import PartitionSpec as P

BLOCK = 256
LANES = 128
FIRST = 160
ROWS_CONTRACT = (((1,), (1,)), ((), ()))
VMEM = pl.BlockSpec(memory_space=pltpu.VMEM)
SMEM = pl.BlockSpec(memory_space=pltpu.SMEM)


def unit_rows(values):
    wide = values.astype(jnp.float32)
    factor = lax.rsqrt(jnp.sum(wide * wide, axis=1, keepdims=True) + 1e-06)
    return (wide * factor).astype(jnp.bfloat16)


def params(flops, bytes_accessed):
    return dict(
        compiler_params=pltpu.CompilerParams(vmem_limit_bytes=16 * 2**20),
        cost_estimate=pl.CostEstimate(flops=flops, bytes_accessed=bytes_accessed, transcendentals=0),
    )


def cut_kernel(emb_ref, second_ref, first_ref):
    second_ref[...] = emb_ref[: BLOCK - FIRST, :]
    first_ref[...] = emb_ref[BLOCK - FIRST :, :]


def normalise_kernel(emb_ref, unit_ref):
    def step(i, _):
        at = pl.multiple_of(i * BLOCK, BLOCK)
        unit_ref[pl.ds(at, BLOCK), :] = unit_rows(emb_ref[pl.ds(at, BLOCK), :])
        return 0

    lax.fori_loop(0, emb_ref.shape[0] // BLOCK, step, 0)


def prepare_kernel(
    slots, own_ref, pairs_ref, fwd_ref, bwd_own_ref, bwd_sibling_ref, unit_ref, fwd_at_ref, bwd_at_ref, listed_ref
):
    src_pos = lax.axis_index("src")
    tgt_pos = lax.axis_index("tgt")
    tgt_count = lax.axis_size("tgt")
    rows = own_ref.shape[0]
    normalise_kernel(own_ref, unit_ref)
    for group in range(fwd_at_ref.shape[0]):
        parts = []
        for g in range(8):
            slot, half = (group * 8 + g) // 2, g % 2
            first = lax.bitwise_xor(tgt_pos, 2 * slot) * BLOCK + half * LANES
            parts.append(fwd_ref[:, pl.ds(pl.multiple_of(first, LANES), LANES)])
        near = jnp.concatenate(parts, axis=0)
        chip = lax.bitwise_xor(near // rows, tgt_pos)
        at = jnp.where(chip < 2, chip * rows + near % rows, -1)
        fwd_at_ref[group] = at.T
    tiles = rows // LANES
    for group in range(bwd_at_ref.shape[0]):
        parts = []
        for g in range(8):
            tile = group * 8 + g
            ref = bwd_own_ref if tile < tiles else bwd_sibling_ref
            parts.append(ref[:, (tile % tiles) * LANES : (tile % tiles + 1) * LANES])
        near = jnp.concatenate(parts, axis=0)
        block = near // BLOCK - src_pos * tgt_count
        inside = (block >= 0) & (block < tgt_count)
        peer = lax.bitwise_xor(jnp.where(inside, block, 0), tgt_pos)
        inside = inside & (lax.bitwise_and(peer, 1) == 0)
        at = jnp.where(inside, (peer // 2) * BLOCK + near % BLOCK, -1)
        bwd_at_ref[group] = at.T
    blocks = 2 * rows // BLOCK
    for slot in range(slots):
        row = lax.bitwise_xor(tgt_pos, 2 * slot)
        named = [pairs_ref[row, k] for k in range(pairs_ref.shape[1])]
        for p in range(blocks):
            owner = lax.bitwise_xor(tgt_pos, p // (blocks // 2))
            block = owner * (blocks // 2) + p % (blocks // 2)
            hit = jnp.int32(0)
            for name in named:
                hit = hit | (name == block).astype(jnp.int32)
            listed_ref[slot * blocks + p] = hit


def gather_lanes(near, mine, first, pieces, got):
    for c, piece in enumerate(pieces):
        got = jnp.where(mine == first + c, jnp.take_along_axis(piece, near & (LANES - 1), axis=1), got)
    return got


def lane_tiles():
    return lax.broadcasted_iota(jnp.int32, (8, LANES), 1) // 16


def score_rows(unit, own_ref, sibling_ref, scores_ref):
    rows = own_ref.shape[0]
    for i, ref in enumerate((own_ref, sibling_ref)):
        scores_ref[:, i * rows : (i + 1) * rows] = lax.dot_general(
            unit, ref[...], ROWS_CONTRACT, preferred_element_type=jnp.float32
        )


def forward_part(slot, unit, own_ref, sibling_ref, fwd_at_ref, scores_ref, got_ref):
    rows = own_ref.shape[0]
    score_rows(unit, own_ref, sibling_ref, scores_ref)
    lane_tile = lane_tiles()
    for at in range(0, LANES, 8):
        near = fwd_at_ref[(2 * slot) // 8, at : at + 8, :]
        got = jnp.zeros((8, LANES), jnp.float32)
        for half in range(2):
            mine = jnp.where(lane_tile == (2 * slot + half) % 8, near >> 7, -1)
            row = half * LANES + at
            pieces = [scores_ref[row : row + 8, c : c + LANES] for c in range(0, 2 * rows, LANES)]
            got = gather_lanes(near, mine, 0, pieces, got)
        got_ref[at : at + 8, :] = got
    first = (2 * slot) % 8 * 16
    return got_ref[...].T[first : first + 32].reshape(2, 16, LANES).sum(axis=1)


def backward_part(slot, unit, own_ref, sibling_ref, bwd_at_ref, turned_ref, got_ref):
    rows = own_ref.shape[0]
    for i, ref in enumerate((own_ref, sibling_ref)):
        turned_ref[i * rows : (i + 1) * rows, :] = lax.dot_general(
            ref[...], unit, ROWS_CONTRACT, preferred_element_type=jnp.float32
        )
    lane_tile = lane_tiles()
    sums = []
    for group in range(bwd_at_ref.shape[0]):
        for at in range(0, LANES, 8):
            near = bwd_at_ref[group, at : at + 8, :]
            got = jnp.zeros((8, LANES), jnp.float32)
            for g in range(8):
                mine = jnp.where(lane_tile == g, near >> 7, -1)
                row = (group * 8 + g) * LANES + at
                pieces = [turned_ref[row : row + 8, c : c + LANES] for c in range(0, BLOCK, LANES)]
                got = gather_lanes(near, mine, 2 * slot, pieces, got)
            got_ref[at : at + 8, :] = got
        sums.append(got_ref[...].T.reshape(8, 16, LANES).sum(axis=1))
    return sums[0] if len(sums) == 1 else jnp.concatenate(sums, axis=0)


def score_kernel(slot, parts, own_ref, sibling_ref, fwd_at_ref, bwd_at_ref, *refs):
    chunk_refs = refs[:parts]
    scores_ref, fwd_ref, bwd_ref, turned_ref, got_ref, back_ref = refs[parts:]
    unit = jnp.concatenate([unit_rows(ref[...]) for ref in chunk_refs], axis=0)
    fwd_ref[...] = forward_part(slot, unit, own_ref, sibling_ref, fwd_at_ref, scores_ref, got_ref)
    bwd_ref[...] = backward_part(slot, unit, own_ref, sibling_ref, bwd_at_ref, turned_ref, back_ref)


def last_first_kernel(slot, parts, own_ref, sibling_ref, fwd_at_ref, bwd_at_ref, *refs):
    chunk_refs, refs = refs[:parts], refs[parts:]
    fwd_before, bwd_before = refs[:slot], refs[slot : 2 * slot]
    unit_ref, scores_ref, send_ref, keep_ref, turned_ref, got_ref = refs[2 * slot :]
    unit_ref[...] = jnp.concatenate([unit_rows(ref[...]) for ref in chunk_refs], axis=0)
    odd = lax.axis_index("tgt") % 2 == 1
    rows = send_ref.shape[0]

    @pl.when(odd)
    def _():
        fwd = forward_part(slot, unit_ref[...], own_ref, sibling_ref, fwd_at_ref, scores_ref, got_ref)
        send_ref[...] = fit(jnp.concatenate([*(ref[...] for ref in fwd_before), fwd], axis=0), rows)

    bwd = backward_part(slot, unit_ref[...], own_ref, sibling_ref, bwd_at_ref, turned_ref, got_ref)
    for ref in bwd_before:
        bwd = bwd + ref[...]
    keep_ref[...] = fit(bwd, rows)

    @pl.when(jnp.logical_not(odd))
    def _():
        send_ref[...] = fit(bwd, rows)


def last_second_kernel(slot, own_ref, sibling_ref, fwd_at_ref, unit_ref, first_scores_ref, *refs):
    fwd_before, (scores_ref, keep_ref, got_ref) = refs[:slot], refs[slot:]
    rows = keep_ref.shape[0]
    odd = lax.axis_index("tgt") % 2 == 1

    @pl.when(odd)
    def _():
        scores_ref[...] = first_scores_ref[...]
        keep_ref[...] = jnp.zeros_like(keep_ref)

    @pl.when(jnp.logical_not(odd))
    def _():
        fwd = forward_part(slot, unit_ref[...], own_ref, sibling_ref, fwd_at_ref, scores_ref, got_ref)
        keep_ref[...] = fit(jnp.concatenate([*(ref[...] for ref in fwd_before), fwd], axis=0), rows)


def fit(value, rows):
    if value.shape[0] < rows:
        value = jnp.concatenate([value, jnp.zeros((rows - value.shape[0], LANES), value.dtype)], axis=0)
    return value[:rows]


def choose(on_odd, on_even, rows):
    odd = lax.broadcasted_iota(jnp.int32, (rows, LANES), 0) * 0 + lax.axis_index("tgt") % 2 == 1
    return jnp.where(odd, fit(on_odd, rows), fit(on_even, rows))


def turn_pair(value):
    half = value.shape[0] // 2
    return jnp.concatenate([value[half:], value[:half]], axis=0)


def masks(slots):
    return [2, 1, *range(3, slots)]


def pair_kernel(combine, by_src_ref, by_tgt_ref, got_ref, state_ref):
    high, wide = by_src_ref.shape[0], by_tgt_ref.shape[0]
    by_src = jnp.concatenate([by_src_ref[...], got_ref[:high, :]], axis=0)
    by_tgt = combine(by_tgt_ref[...], turn_pair(got_ref[:wide, :]))
    state_ref[...] = choose(by_tgt, by_src, state_ref.shape[0])


def pair_kept_kernel(high, wide, by_tgt_ref, by_src_ref, got_ref, state_ref):
    by_src = jnp.concatenate([by_src_ref[:high, :], got_ref[:high, :]], axis=0)
    by_tgt = by_tgt_ref[:wide, :] + turn_pair(got_ref[:wide, :])
    state_ref[...] = choose(by_tgt, by_src, state_ref.shape[0])


def collect_kernel(combine, slots, wide, last, state_ref, *refs):
    got_refs, (total_ref, send_ref) = refs[:-2], refs[-2:]
    by_tgt = state_ref[:wide, :]
    by_src = [state_ref[2 * i : 2 * i + 2, :] for i in range(2 * slots)]
    for k, ref in enumerate(got_refs):
        by_tgt = combine(by_tgt, ref[:wide, :])
        if k + 1 < slots:
            order = [2 * (i ^ masks(slots)[k]) for i in range(2 * slots)]
            by_src = [combine(one, ref[i : i + 2, :]) for one, i in zip(by_src, order, strict=True)]
    by_src = jnp.concatenate(by_src, axis=0)
    total_ref[...] = choose(by_tgt, by_src, total_ref.shape[0])
    send_ref[...] = choose(by_tgt[wide // 2 :] if last else by_tgt, by_src[2 * slots :], send_ref.shape[0])


def widen_kernel(wide, total_ref, got_ref, wide_ref, bwd_ref):
    high = wide_ref.shape[0] // LANES
    fwd = choose(got_ref[:high, :], total_ref[:high, :], high)
    bwd_ref[...] = choose(total_ref[:wide, :], turn_pair(got_ref[:wide, :]), wide)
    for g in range(high):
        wide_ref[g * LANES : (g + 1) * LANES, :] = jnp.broadcast_to(fwd[g : g + 1, :], (LANES, LANES)).T


def margin_kernel(slots, columns, *refs):
    score_refs = refs[:slots]
    wide_ref, bwd_ref, listed_ref, src_ref, tgt_ref, send_ref, row_ref, col_ref = refs[slots:]
    blocks = columns // BLOCK
    row_ref[...] = jnp.zeros_like(row_ref)
    col_ref[...] = jnp.zeros_like(col_ref)

    for slot in range(slots):
        scores_ref = score_refs[slot]

        def tile(p, _, slot=slot, scores_ref=scores_ref):
            @pl.when(listed_ref[slot * blocks + p] != 0)
            def _():
                columns_at = [pl.ds(pl.multiple_of(p * BLOCK + c * LANES, LANES), LANES) for c in range(2)]
                bwd = [jnp.broadcast_to(bwd_ref[pl.ds(2 * p + c, 1), :], (8, LANES)) for c in range(2)]
                peak = [jnp.zeros((8, LANES), jnp.float32)] * 2
                for at in range(0, BLOCK, 8):
                    rows = slice(slot * BLOCK + at, slot * BLOCK + at + 8)
                    fwd = wide_ref[rows, :]
                    best = row_ref[rows, :]
                    for c in range(2):
                        total = fwd + bwd[c]
                        inverse = pl.reciprocal(total, approx=True)
                        inverse = inverse * (2.0 - total * inverse)
                        ratio = scores_ref[at : at + 8, columns_at[c]] * inverse
                        best = jnp.maximum(best, ratio)
                        peak[c] = jnp.maximum(peak[c], ratio)
                    row_ref[rows, :] = best
                for c in range(2):
                    col_ref[:, columns_at[c]] = jnp.maximum(col_ref[:, columns_at[c]], peak[c])

            return 0

        lax.fori_loop(0, blocks, tile, 0)
    for c in range(columns // LANES):
        tgt_ref[c : c + 1, :] = 32.0 * jnp.max(col_ref[:, c * LANES : (c + 1) * LANES], axis=0, keepdims=True)
    for g in range(src_ref.shape[0]):
        src_ref[g : g + 1, :] = 32.0 * jnp.max(row_ref[g * LANES : (g + 1) * LANES, :].T, axis=0, keepdims=True)
    send_ref[...] = choose(src_ref[...], tgt_ref[...], send_ref.shape[0])


def last_kernel(total_ref, got_ref, src_ref, tgt_ref):
    src, tgt = src_ref.shape[0], tgt_ref.shape[0]
    src_ref[...] = choose(got_ref[:src, :], total_ref[:src, :], src)
    tgt_ref[...] = choose(total_ref[:tgt, :], got_ref[:tgt, :], tgt)


def swap(value, axis, mask):
    count = lax.axis_size(axis)
    return lax.ppermute(value, axis, [(i, i ^ mask) for i in range(count)])


def small_call(kernel, name, shapes, *args):
    return pl.pallas_call(
        kernel,
        out_shape=tuple(jax.ShapeDtypeStruct((rows, LANES), jnp.float32) for rows in shapes),
        in_specs=[VMEM] * len(args),
        out_specs=(VMEM,) * len(shapes),
        name=name,
        **params(10**6, 10**6),
    )(*args)


def reduce_all(combine, high, wide, state, name, last):
    tgt_count, src_count = lax.axis_size("tgt"), lax.axis_size("src")
    parts = []
    for i in range(1, max(tgt_count // 2, src_count)):
        pairs = []
        for device in range(src_count * tgt_count):
            if device % 2 == 0 and i < tgt_count // 2:
                pairs.append((device, device ^ (2 * masks(tgt_count // 2)[i - 1])))
            if device % 2 == 1 and i < src_count:
                pairs.append((device, device ^ (i * tgt_count)))
        parts.append(lax.ppermute(state, ("src", "tgt"), pairs))
    back = max(2, wide // 2) if last else max(high, wide)
    total, send = small_call(
        functools.partial(collect_kernel, combine, high // 2, wide, last), name, (state.shape[0], back), state, *parts
    )
    return total, swap(send, "tgt", 1)


def body(src_emb, tgt_emb, pair_list, fwd_idx, bwd_idx):
    tgt_count = lax.axis_size("tgt")
    slots = tgt_count // 2
    rows, width = tgt_emb.shape
    columns = 2 * rows
    tgt_bits = [1 << b for b in range(1, tgt_count.bit_length() - 1)]

    along_x = swap(src_emb, "tgt", 2)
    second, first = pl.pallas_call(
        cut_kernel,
        out_shape=(
            jax.ShapeDtypeStruct((BLOCK - FIRST, width), src_emb.dtype),
            jax.ShapeDtypeStruct((FIRST, width), src_emb.dtype),
        ),
        in_specs=[VMEM],
        out_specs=(VMEM, VMEM),
        name="cut",
        **params(1000, 1000),
    )(src_emb)
    y_first = swap(first, "tgt", 4)

    sibling_emb = swap(tgt_emb, "tgt", 1)
    bwd_lists = bwd_idx.T
    sibling_lists = swap(bwd_lists, "tgt", 1)

    bwd_shape = jax.ShapeDtypeStruct((columns // (8 * LANES), LANES, LANES), jnp.int32)
    unit_shape = jax.ShapeDtypeStruct((rows, width), jnp.bfloat16)
    sibling_unit = pl.pallas_call(
        normalise_kernel,
        out_shape=unit_shape,
        in_specs=[VMEM],
        out_specs=VMEM,
        name="normalise",
        **params(10**9, rows * width * 4),
    )(sibling_emb)
    own_unit, fwd_at, bwd_at, listed = pl.pallas_call(
        functools.partial(prepare_kernel, slots),
        out_shape=(
            unit_shape,
            jax.ShapeDtypeStruct((-(-slots // 4), LANES, LANES), jnp.int32),
            bwd_shape,
            jax.ShapeDtypeStruct((slots * columns // BLOCK,), jnp.int32),
        ),
        in_specs=[VMEM, SMEM, VMEM, VMEM, VMEM],
        out_specs=(VMEM, VMEM, VMEM, SMEM),
        name="prepare",
        **params(1000, 1000),
    )(tgt_emb, pair_list, fwd_idx.T, bwd_lists, sibling_lists)

    scores_shape = jax.ShapeDtypeStruct((BLOCK, columns), jnp.float32)
    bwd_sums = jax.ShapeDtypeStruct((columns // LANES, LANES), jnp.float32)
    turned = pltpu.VMEM((columns, BLOCK), jnp.float32)
    got = pltpu.VMEM((LANES, LANES), jnp.float32)

    def score(slot, parts):
        args = [own_unit, sibling_unit, fwd_at, bwd_at, *parts]
        return pl.pallas_call(
            functools.partial(score_kernel, slot, len(parts)),
            out_shape=(scores_shape, jax.ShapeDtypeStruct((2, LANES), jnp.float32), bwd_sums),
            in_specs=[VMEM] * len(args),
            out_specs=(VMEM, VMEM, VMEM),
            scratch_shapes=[turned, got, got],
            name=f"score_{slot}",
            **(params(4 * BLOCK * columns * width, BLOCK * columns * 4) if slot else params(1000, 1000)),
        )(*args)

    own_unit, sibling_unit = lax.optimization_barrier((own_unit, sibling_unit))
    y_second = swap(second, "tgt", 4)
    done = [score(0, (src_emb,))]
    y_first, *done[0] = lax.optimization_barrier((y_first, *done[0]))
    far_first = swap(y_first, "tgt", 2)
    along_x, *done[0] = lax.optimization_barrier((along_x, *done[0]))
    far_second = swap(along_x[: BLOCK - FIRST], "tgt", 4)
    blocks = [(src_emb,), (along_x,), (y_second, y_first), (far_second, far_first)]
    for bit in tgt_bits[2:]:
        blocks += [tuple(swap(part, "tgt", bit) for part in held) for held in blocks]
    along_y = score(2, blocks[2])
    along_x, *along_y = lax.optimization_barrier((along_x, *along_y))
    done += [score(1, (along_x,)), along_y]
    for slot in range(3, slots - 1):
        done.append(score(slot, blocks[slot]))
    high, wide = 2 * slots, columns // LANES
    sent = jax.ShapeDtypeStruct((max(high, wide), LANES), jnp.float32)
    before = [*(d[1] for d in done), *(d[2] for d in done)]
    args = [own_unit, sibling_unit, fwd_at, bwd_at, *blocks[-1], *before]
    last_unit, last_scores, send, keep_tgt = pl.pallas_call(
        functools.partial(last_first_kernel, slots - 1, len(blocks[-1])),
        out_shape=(jax.ShapeDtypeStruct((BLOCK, width), jnp.bfloat16), scores_shape, sent, sent),
        in_specs=[VMEM] * len(args),
        out_specs=(VMEM,) * 4,
        scratch_shapes=[turned, got],
        name="last_first",
        **params(2 * BLOCK * columns * width, BLOCK * columns * 4),
    )(*args)
    got_sums = swap(send, "tgt", 1)
    args = [own_unit, sibling_unit, fwd_at, last_unit, last_scores, *(d[1] for d in done)]
    last_scores, keep_src = pl.pallas_call(
        functools.partial(last_second_kernel, slots - 1),
        out_shape=(scores_shape, sent),
        in_specs=[VMEM] * len(args),
        out_specs=(VMEM, VMEM),
        input_output_aliases={4: 0},
        scratch_shapes=[got],
        name="last_second",
        **params(2 * BLOCK * columns * width, BLOCK * columns * 4),
    )(*args)
    scores = [*(d[0] for d in done), last_scores]

    state_rows = max(2 * high, wide)
    (state,) = small_call(
        functools.partial(pair_kept_kernel, high, wide), "mean_pair", (state_rows,), keep_tgt, keep_src, got_sums
    )
    total, got_sums = reduce_all(jnp.add, high, wide, state, "mean_collect", False)
    wide_fwd, bwd = small_call(functools.partial(widen_kernel, wide), "widen", (slots * BLOCK, wide), total, got_sums)
    src_best, tgt_best, send = pl.pallas_call(
        functools.partial(margin_kernel, slots, columns),
        out_shape=(jax.ShapeDtypeStruct((high, LANES), jnp.float32), bwd_sums, sent),
        in_specs=[VMEM] * (slots + 2) + [SMEM],
        out_specs=(VMEM,) * 3,
        scratch_shapes=[pltpu.VMEM((slots * BLOCK, LANES), jnp.float32), pltpu.VMEM((8, columns), jnp.float32)],
        name="margins",
        **params(slots * BLOCK * columns * 10, slots * BLOCK * columns * 4),
    )(*scores, wide_fwd, bwd, listed)
    got_best = swap(send, "tgt", 1)
    (state,) = small_call(
        functools.partial(pair_kernel, jnp.maximum), "best_pair", (state_rows,), src_best, tgt_best, got_best
    )
    total, got_best = reduce_all(jnp.maximum, high, wide, state, "best_collect", True)
    src_best, tgt_best = small_call(last_kernel, "last", (BLOCK // LANES, rows // LANES), total, got_best)
    return src_best.reshape(-1), tgt_best.reshape(-1)


def solution(mesh):
    return jax.shard_map(
        body,
        mesh=mesh,
        in_specs=(
            P(("src", "tgt"), None),
            P("tgt", None),
            P("src", None),
            P("src", None),
            P("tgt", None),
        ),
        out_specs=(P(("src", "tgt")), P("tgt")),
        check_vma=False,
    )
```

```python
import functools

import jax
import jax.numpy as jnp
from jax import lax
from jax.experimental import pallas as pl
from jax.experimental.pallas import tpu as pltpu
from jax.sharding import PartitionSpec as P

BLOCK = 256
LANES = 128
FIRST = 160
ROWS_CONTRACT = (((1,), (1,)), ((), ()))
VMEM = pl.BlockSpec(memory_space=pltpu.VMEM)
SMEM = pl.BlockSpec(memory_space=pltpu.SMEM)


def unit_rows(values):
    wide = values.astype(jnp.float32)
    factor = lax.rsqrt(jnp.sum(wide * wide, axis=1, keepdims=True) + 1e-06)
    return (wide * factor).astype(jnp.bfloat16)


def params(flops, bytes_accessed):
    return dict(
        compiler_params=pltpu.CompilerParams(vmem_limit_bytes=16 * 2**20),
        cost_estimate=pl.CostEstimate(flops=flops, bytes_accessed=bytes_accessed, transcendentals=0),
    )


def cut_kernel(emb_ref, second_ref, first_ref):
    second_ref[...] = emb_ref[: BLOCK - FIRST, :]
    first_ref[...] = emb_ref[BLOCK - FIRST :, :]


def normalise_kernel(emb_ref, unit_ref):
    def step(i, _):
        at = pl.multiple_of(i * BLOCK, BLOCK)
        unit_ref[pl.ds(at, BLOCK), :] = unit_rows(emb_ref[pl.ds(at, BLOCK), :])
        return 0

    lax.fori_loop(0, emb_ref.shape[0] // BLOCK, step, 0)


def prepare_kernel(
    slots, own_ref, pairs_ref, fwd_ref, bwd_own_ref, bwd_sibling_ref, unit_ref, fwd_at_ref, bwd_at_ref, listed_ref
):
    src_pos = lax.axis_index("src")
    tgt_pos = lax.axis_index("tgt")
    tgt_count = lax.axis_size("tgt")
    rows = own_ref.shape[0]
    normalise_kernel(own_ref, unit_ref)
    for group in range(fwd_at_ref.shape[0]):
        parts = []
        for g in range(8):
            slot, half = (group * 8 + g) // 2, g % 2
            first = lax.bitwise_xor(tgt_pos, 2 * slot) * BLOCK + half * LANES
            parts.append(fwd_ref[:, pl.ds(pl.multiple_of(first, LANES), LANES)])
        near = jnp.concatenate(parts, axis=0)
        chip = lax.bitwise_xor(near // rows, tgt_pos)
        at = jnp.where(chip < 2, chip * rows + near % rows, -1)
        fwd_at_ref[group] = at.T
    tiles = rows // LANES
    for group in range(bwd_at_ref.shape[0]):
        parts = []
        for g in range(8):
            tile = group * 8 + g
            ref = bwd_own_ref if tile < tiles else bwd_sibling_ref
            parts.append(ref[:, (tile % tiles) * LANES : (tile % tiles + 1) * LANES])
        near = jnp.concatenate(parts, axis=0)
        block = near // BLOCK - src_pos * tgt_count
        inside = (block >= 0) & (block < tgt_count)
        peer = lax.bitwise_xor(jnp.where(inside, block, 0), tgt_pos)
        inside = inside & (lax.bitwise_and(peer, 1) == 0)
        at = jnp.where(inside, (peer // 2) * BLOCK + near % BLOCK, -1)
        bwd_at_ref[group] = at.T
    blocks = 2 * rows // BLOCK
    for slot in range(slots):
        row = lax.bitwise_xor(tgt_pos, 2 * slot)
        named = [pairs_ref[row, k] for k in range(pairs_ref.shape[1])]
        for p in range(blocks):
            owner = lax.bitwise_xor(tgt_pos, p // (blocks // 2))
            block = owner * (blocks // 2) + p % (blocks // 2)
            hit = jnp.int32(0)
            for name in named:
                hit = hit | (name == block).astype(jnp.int32)
            listed_ref[slot * blocks + p] = hit


def gather_lanes(near, mine, first, pieces, got):
    for c, piece in enumerate(pieces):
        got = jnp.where(mine == first + c, jnp.take_along_axis(piece, near & (LANES - 1), axis=1), got)
    return got


def lane_tiles():
    return lax.broadcasted_iota(jnp.int32, (8, LANES), 1) // 16


def score_rows(unit, own_ref, sibling_ref, scores_ref):
    rows = own_ref.shape[0]
    for i, ref in enumerate((own_ref, sibling_ref)):
        scores_ref[:, i * rows : (i + 1) * rows] = lax.dot_general(
            unit, ref[...], ROWS_CONTRACT, preferred_element_type=jnp.float32
        )


def forward_part(slot, unit, own_ref, sibling_ref, fwd_at_ref, scores_ref, got_ref):
    rows = own_ref.shape[0]
    score_rows(unit, own_ref, sibling_ref, scores_ref)
    lane_tile = lane_tiles()
    for at in range(0, LANES, 8):
        near = fwd_at_ref[(2 * slot) // 8, at : at + 8, :]
        got = jnp.zeros((8, LANES), jnp.float32)
        for half in range(2):
            mine = jnp.where(lane_tile == (2 * slot + half) % 8, near >> 7, -1)
            row = half * LANES + at
            pieces = [scores_ref[row : row + 8, c : c + LANES] for c in range(0, 2 * rows, LANES)]
            got = gather_lanes(near, mine, 0, pieces, got)
        got_ref[at : at + 8, :] = got
    first = (2 * slot) % 8 * 16
    return got_ref[...].T[first : first + 32].reshape(2, 16, LANES).sum(axis=1)


def backward_part(slot, unit, own_ref, sibling_ref, bwd_at_ref, turned_ref, got_ref):
    rows = own_ref.shape[0]
    for i, ref in enumerate((own_ref, sibling_ref)):
        turned_ref[i * rows : (i + 1) * rows, :] = lax.dot_general(
            ref[...], unit, ROWS_CONTRACT, preferred_element_type=jnp.float32
        )
    lane_tile = lane_tiles()
    sums = []
    for group in range(bwd_at_ref.shape[0]):
        for at in range(0, LANES, 8):
            near = bwd_at_ref[group, at : at + 8, :]
            got = jnp.zeros((8, LANES), jnp.float32)
            for g in range(8):
                mine = jnp.where(lane_tile == g, near >> 7, -1)
                row = (group * 8 + g) * LANES + at
                pieces = [turned_ref[row : row + 8, c : c + LANES] for c in range(0, BLOCK, LANES)]
                got = gather_lanes(near, mine, 2 * slot, pieces, got)
            got_ref[at : at + 8, :] = got
        sums.append(got_ref[...].T.reshape(8, 16, LANES).sum(axis=1))
    return sums[0] if len(sums) == 1 else jnp.concatenate(sums, axis=0)


def score_kernel(slot, parts, own_ref, sibling_ref, fwd_at_ref, bwd_at_ref, *refs):
    chunk_refs = refs[:parts]
    scores_ref, fwd_ref, bwd_ref, turned_ref, got_ref, back_ref = refs[parts:]
    unit = jnp.concatenate([unit_rows(ref[...]) for ref in chunk_refs], axis=0)
    fwd_ref[...] = forward_part(slot, unit, own_ref, sibling_ref, fwd_at_ref, scores_ref, got_ref)
    bwd_ref[...] = backward_part(slot, unit, own_ref, sibling_ref, bwd_at_ref, turned_ref, back_ref)


def last_first_kernel(slot, parts, own_ref, sibling_ref, fwd_at_ref, bwd_at_ref, *refs):
    chunk_refs, refs = refs[:parts], refs[parts:]
    fwd_before, bwd_before = refs[:slot], refs[slot : 2 * slot]
    unit_ref, scores_ref, send_ref, keep_ref, turned_ref, got_ref = refs[2 * slot :]
    unit_ref[...] = jnp.concatenate([unit_rows(ref[...]) for ref in chunk_refs], axis=0)
    odd = lax.axis_index("tgt") % 2 == 1
    rows = send_ref.shape[0]

    @pl.when(odd)
    def _():
        fwd = forward_part(slot, unit_ref[...], own_ref, sibling_ref, fwd_at_ref, scores_ref, got_ref)
        send_ref[...] = fit(jnp.concatenate([*(ref[...] for ref in fwd_before), fwd], axis=0), rows)

    bwd = backward_part(slot, unit_ref[...], own_ref, sibling_ref, bwd_at_ref, turned_ref, got_ref)
    for ref in bwd_before:
        bwd = bwd + ref[...]
    keep_ref[...] = fit(bwd, rows)

    @pl.when(jnp.logical_not(odd))
    def _():
        send_ref[...] = fit(bwd, rows)


def last_second_kernel(slot, own_ref, sibling_ref, fwd_at_ref, unit_ref, first_scores_ref, *refs):
    fwd_before, (scores_ref, keep_ref, got_ref) = refs[:slot], refs[slot:]
    rows = keep_ref.shape[0]
    odd = lax.axis_index("tgt") % 2 == 1

    @pl.when(odd)
    def _():
        scores_ref[...] = first_scores_ref[...]
        keep_ref[...] = jnp.zeros_like(keep_ref)

    @pl.when(jnp.logical_not(odd))
    def _():
        fwd = forward_part(slot, unit_ref[...], own_ref, sibling_ref, fwd_at_ref, scores_ref, got_ref)
        keep_ref[...] = fit(jnp.concatenate([*(ref[...] for ref in fwd_before), fwd], axis=0), rows)


def fit(value, rows):
    if value.shape[0] < rows:
        value = jnp.concatenate([value, jnp.zeros((rows - value.shape[0], LANES), value.dtype)], axis=0)
    return value[:rows]


def choose(on_odd, on_even, rows):
    odd = lax.broadcasted_iota(jnp.int32, (rows, LANES), 0) * 0 + lax.axis_index("tgt") % 2 == 1
    return jnp.where(odd, fit(on_odd, rows), fit(on_even, rows))


def turn_pair(value):
    half = value.shape[0] // 2
    return jnp.concatenate([value[half:], value[:half]], axis=0)


def masks(slots):
    return [2, 1, *range(3, slots)]


def pair_kernel(combine, by_src_ref, by_tgt_ref, got_ref, state_ref):
    high, wide = by_src_ref.shape[0], by_tgt_ref.shape[0]
    by_src = jnp.concatenate([by_src_ref[...], got_ref[:high, :]], axis=0)
    by_tgt = combine(by_tgt_ref[...], turn_pair(got_ref[:wide, :]))
    state_ref[...] = choose(by_tgt, by_src, state_ref.shape[0])


def pair_kept_kernel(high, wide, by_tgt_ref, by_src_ref, got_ref, state_ref):
    by_src = jnp.concatenate([by_src_ref[:high, :], got_ref[:high, :]], axis=0)
    by_tgt = by_tgt_ref[:wide, :] + turn_pair(got_ref[:wide, :])
    state_ref[...] = choose(by_tgt, by_src, state_ref.shape[0])


def collect_kernel(combine, slots, wide, last, state_ref, *refs):
    got_refs, (total_ref, send_ref) = refs[:-2], refs[-2:]
    by_tgt = state_ref[:wide, :]
    by_src = [state_ref[2 * i : 2 * i + 2, :] for i in range(2 * slots)]
    for k, ref in enumerate(got_refs):
        by_tgt = combine(by_tgt, ref[:wide, :])
        if k + 1 < slots:
            order = [2 * (i ^ masks(slots)[k]) for i in range(2 * slots)]
            by_src = [combine(one, ref[i : i + 2, :]) for one, i in zip(by_src, order, strict=True)]
    by_src = jnp.concatenate(by_src, axis=0)
    total_ref[...] = choose(by_tgt, by_src, total_ref.shape[0])
    send_ref[...] = choose(by_tgt[wide // 2 :] if last else by_tgt, by_src[2 * slots :], send_ref.shape[0])


def widen(fwd, wide_ref):
    for g in range(fwd.shape[0]):
        wide_ref[g * LANES : (g + 1) * LANES, :] = jnp.broadcast_to(fwd[g : g + 1, :], (LANES, LANES)).T


def widen_own_kernel(total_ref, wide_ref):
    @pl.when(lax.axis_index("tgt") % 2 == 0)
    def _():
        widen(total_ref[: wide_ref.shape[0] // LANES, :], wide_ref)

    @pl.when(lax.axis_index("tgt") % 2 == 1)
    def _():
        wide_ref[...] = jnp.zeros_like(wide_ref)


def widen_kernel(wide, total_ref, got_ref, own_wide_ref, wide_ref, bwd_ref):
    bwd_ref[...] = choose(total_ref[:wide, :], turn_pair(got_ref[:wide, :]), wide)

    @pl.when(lax.axis_index("tgt") % 2 == 1)
    def _():
        widen(got_ref[: wide_ref.shape[0] // LANES, :], wide_ref)

    @pl.when(lax.axis_index("tgt") % 2 == 0)
    def _():
        wide_ref[...] = own_wide_ref[...]


def margin_kernel(slots, columns, *refs):
    score_refs = refs[:slots]
    wide_ref, bwd_ref, listed_ref, src_ref, tgt_ref, send_ref, row_ref, col_ref = refs[slots:]
    blocks = columns // BLOCK
    row_ref[...] = jnp.zeros_like(row_ref)
    col_ref[...] = jnp.zeros_like(col_ref)

    for slot in range(slots):
        scores_ref = score_refs[slot]

        def tile(p, _, slot=slot, scores_ref=scores_ref):
            @pl.when(listed_ref[slot * blocks + p] != 0)
            def _():
                columns_at = [pl.ds(pl.multiple_of(p * BLOCK + c * LANES, LANES), LANES) for c in range(2)]
                bwd = [jnp.broadcast_to(bwd_ref[pl.ds(2 * p + c, 1), :], (8, LANES)) for c in range(2)]
                peak = [jnp.zeros((8, LANES), jnp.float32)] * 2
                for at in range(0, BLOCK, 8):
                    rows = slice(slot * BLOCK + at, slot * BLOCK + at + 8)
                    fwd = wide_ref[rows, :]
                    best = row_ref[rows, :]
                    for c in range(2):
                        total = fwd + bwd[c]
                        inverse = pl.reciprocal(total, approx=True)
                        inverse = inverse * (2.0 - total * inverse)
                        ratio = scores_ref[at : at + 8, columns_at[c]] * inverse
                        best = jnp.maximum(best, ratio)
                        peak[c] = jnp.maximum(peak[c], ratio)
                    row_ref[rows, :] = best
                for c in range(2):
                    col_ref[:, columns_at[c]] = jnp.maximum(col_ref[:, columns_at[c]], peak[c])

            return 0

        lax.fori_loop(0, blocks, tile, 0)
    for c in range(columns // LANES):
        tgt_ref[c : c + 1, :] = 32.0 * jnp.max(col_ref[:, c * LANES : (c + 1) * LANES], axis=0, keepdims=True)
    for g in range(src_ref.shape[0]):
        src_ref[g : g + 1, :] = 32.0 * jnp.max(row_ref[g * LANES : (g + 1) * LANES, :].T, axis=0, keepdims=True)
    send_ref[...] = choose(src_ref[...], tgt_ref[...], send_ref.shape[0])


def last_kernel(total_ref, got_ref, src_ref, tgt_ref):
    src, tgt = src_ref.shape[0], tgt_ref.shape[0]
    src_ref[...] = choose(got_ref[:src, :], total_ref[:src, :], src)
    tgt_ref[...] = choose(total_ref[:tgt, :], got_ref[:tgt, :], tgt)


def swap(value, axis, mask):
    count = lax.axis_size(axis)
    return lax.ppermute(value, axis, [(i, i ^ mask) for i in range(count)])


def small_call(kernel, name, shapes, *args):
    return pl.pallas_call(
        kernel,
        out_shape=tuple(jax.ShapeDtypeStruct((rows, LANES), jnp.float32) for rows in shapes),
        in_specs=[VMEM] * len(args),
        out_specs=(VMEM,) * len(shapes),
        name=name,
        **params(10**6, 10**6),
    )(*args)


def reduce_all(combine, high, wide, state, name, last):
    tgt_count, src_count = lax.axis_size("tgt"), lax.axis_size("src")
    parts = []
    for i in range(1, max(tgt_count // 2, src_count)):
        pairs = []
        for device in range(src_count * tgt_count):
            if device % 2 == 0 and i < tgt_count // 2:
                pairs.append((device, device ^ (2 * masks(tgt_count // 2)[i - 1])))
            if device % 2 == 1 and i < src_count:
                pairs.append((device, device ^ (i * tgt_count)))
        parts.append(lax.ppermute(state, ("src", "tgt"), pairs))
    back = max(2, wide // 2) if last else max(high, wide)
    total, send = small_call(
        functools.partial(collect_kernel, combine, high // 2, wide, last), name, (state.shape[0], back), state, *parts
    )
    return total, swap(send, "tgt", 1)


def body(src_emb, tgt_emb, pair_list, fwd_idx, bwd_idx):
    tgt_count = lax.axis_size("tgt")
    slots = tgt_count // 2
    rows, width = tgt_emb.shape
    columns = 2 * rows
    tgt_bits = [1 << b for b in range(1, tgt_count.bit_length() - 1)]

    along_x = swap(src_emb, "tgt", 2)
    second, first = pl.pallas_call(
        cut_kernel,
        out_shape=(
            jax.ShapeDtypeStruct((BLOCK - FIRST, width), src_emb.dtype),
            jax.ShapeDtypeStruct((FIRST, width), src_emb.dtype),
        ),
        in_specs=[VMEM],
        out_specs=(VMEM, VMEM),
        name="cut",
        **params(1000, 1000),
    )(src_emb)
    y_first = swap(first, "tgt", 4)

    sibling_emb = swap(tgt_emb, "tgt", 1)
    bwd_lists = bwd_idx.T
    sibling_lists = swap(bwd_lists, "tgt", 1)

    bwd_shape = jax.ShapeDtypeStruct((columns // (8 * LANES), LANES, LANES), jnp.int32)
    unit_shape = jax.ShapeDtypeStruct((rows, width), jnp.bfloat16)
    sibling_unit = pl.pallas_call(
        normalise_kernel,
        out_shape=unit_shape,
        in_specs=[VMEM],
        out_specs=VMEM,
        name="normalise",
        **params(10**9, rows * width * 4),
    )(sibling_emb)
    own_unit, fwd_at, bwd_at, listed = pl.pallas_call(
        functools.partial(prepare_kernel, slots),
        out_shape=(
            unit_shape,
            jax.ShapeDtypeStruct((-(-slots // 4), LANES, LANES), jnp.int32),
            bwd_shape,
            jax.ShapeDtypeStruct((slots * columns // BLOCK,), jnp.int32),
        ),
        in_specs=[VMEM, SMEM, VMEM, VMEM, VMEM],
        out_specs=(VMEM, VMEM, VMEM, SMEM),
        name="prepare",
        **params(1000, 1000),
    )(tgt_emb, pair_list, fwd_idx.T, bwd_lists, sibling_lists)

    scores_shape = jax.ShapeDtypeStruct((BLOCK, columns), jnp.float32)
    bwd_sums = jax.ShapeDtypeStruct((columns // LANES, LANES), jnp.float32)
    turned = pltpu.VMEM((columns, BLOCK), jnp.float32)
    got = pltpu.VMEM((LANES, LANES), jnp.float32)

    def score(slot, parts):
        args = [own_unit, sibling_unit, fwd_at, bwd_at, *parts]
        return pl.pallas_call(
            functools.partial(score_kernel, slot, len(parts)),
            out_shape=(scores_shape, jax.ShapeDtypeStruct((2, LANES), jnp.float32), bwd_sums),
            in_specs=[VMEM] * len(args),
            out_specs=(VMEM, VMEM, VMEM),
            scratch_shapes=[turned, got, got],
            name=f"score_{slot}",
            **(params(4 * BLOCK * columns * width, BLOCK * columns * 4) if slot else params(1000, 1000)),
        )(*args)

    own_unit, sibling_unit = lax.optimization_barrier((own_unit, sibling_unit))
    y_second = swap(second, "tgt", 4)
    done = [score(0, (src_emb,))]
    y_first, *done[0] = lax.optimization_barrier((y_first, *done[0]))
    far_first = swap(y_first, "tgt", 2)
    along_x, *done[0] = lax.optimization_barrier((along_x, *done[0]))
    far_second = swap(along_x[: BLOCK - FIRST], "tgt", 4)
    blocks = [(src_emb,), (along_x,), (y_second, y_first), (far_second, far_first)]
    for bit in tgt_bits[2:]:
        blocks += [tuple(swap(part, "tgt", bit) for part in held) for held in blocks]
    along_y = score(2, blocks[2])
    along_x, *along_y = lax.optimization_barrier((along_x, *along_y))
    done += [score(1, (along_x,)), along_y]
    for slot in range(3, slots - 1):
        done.append(score(slot, blocks[slot]))
    high, wide = 2 * slots, columns // LANES
    sent = jax.ShapeDtypeStruct((max(high, wide), LANES), jnp.float32)
    before = [*(d[1] for d in done), *(d[2] for d in done)]
    args = [own_unit, sibling_unit, fwd_at, bwd_at, *blocks[-1], *before]
    last_unit, last_scores, send, keep_tgt = pl.pallas_call(
        functools.partial(last_first_kernel, slots - 1, len(blocks[-1])),
        out_shape=(jax.ShapeDtypeStruct((BLOCK, width), jnp.bfloat16), scores_shape, sent, sent),
        in_specs=[VMEM] * len(args),
        out_specs=(VMEM,) * 4,
        scratch_shapes=[turned, got],
        name="last_first",
        **params(2 * BLOCK * columns * width, BLOCK * columns * 4),
    )(*args)
    got_sums = swap(send, "tgt", 1)
    args = [own_unit, sibling_unit, fwd_at, last_unit, last_scores, *(d[1] for d in done)]
    last_scores, keep_src = pl.pallas_call(
        functools.partial(last_second_kernel, slots - 1),
        out_shape=(scores_shape, sent),
        in_specs=[VMEM] * len(args),
        out_specs=(VMEM, VMEM),
        input_output_aliases={4: 0},
        scratch_shapes=[got],
        name="last_second",
        **params(2 * BLOCK * columns * width, BLOCK * columns * 4),
    )(*args)
    scores = [*(d[0] for d in done), last_scores]

    state_rows = max(2 * high, wide)
    (state,) = small_call(
        functools.partial(pair_kept_kernel, high, wide), "mean_pair", (state_rows,), keep_tgt, keep_src, got_sums
    )
    total, got_sums = reduce_all(jnp.add, high, wide, state, "mean_collect", False)
    (own_wide,) = small_call(widen_own_kernel, "widen_own", (slots * BLOCK,), total)
    wide_fwd, bwd = small_call(
        functools.partial(widen_kernel, wide), "widen", (slots * BLOCK, wide), total, got_sums, own_wide
    )
    src_best, tgt_best, send = pl.pallas_call(
        functools.partial(margin_kernel, slots, columns),
        out_shape=(jax.ShapeDtypeStruct((high, LANES), jnp.float32), bwd_sums, sent),
        in_specs=[VMEM] * (slots + 2) + [SMEM],
        out_specs=(VMEM,) * 3,
        scratch_shapes=[pltpu.VMEM((slots * BLOCK, LANES), jnp.float32), pltpu.VMEM((8, columns), jnp.float32)],
        name="margins",
        **params(slots * BLOCK * columns * 10, slots * BLOCK * columns * 4),
    )(*scores, wide_fwd, bwd, listed)
    got_best = swap(send, "tgt", 1)
    (state,) = small_call(
        functools.partial(pair_kernel, jnp.maximum), "best_pair", (state_rows,), src_best, tgt_best, got_best
    )
    total, got_best = reduce_all(jnp.maximum, high, wide, state, "best_collect", True)
    src_best, tgt_best = small_call(last_kernel, "last", (BLOCK // LANES, rows // LANES), total, got_best)
    return src_best.reshape(-1), tgt_best.reshape(-1)


def solution(mesh):
    return jax.shard_map(
        body,
        mesh=mesh,
        in_specs=(
            P(("src", "tgt"), None),
            P("tgt", None),
            P("src", None),
            P("src", None),
            P("tgt", None),
        ),
        out_specs=(P(("src", "tgt")), P("tgt")),
        check_vma=False,
    )
```
